128 devices in a mesh: row: 8 (over x_hi, y), diag: 16 (over z, x_lo, core).
Axes of the slice: x: 4 (x_hi: 2, x_lo: 2; x = x_hi * 2 + x_lo), y: 4, z: 4, core: 2. Of those that a mesh axis runs over, the one named last changes fastest.
Arguments:
- bins_x: bfloat16 [8192, 256], P(('row', 'diag')), may hold values from -6 to 6
- proj_weight: bfloat16 [256, 64], replicated, may hold values from -0.375 to 0.375
- convolution_weight: bfloat16 [9, 32, 32], replicated, may hold values from -0.375 to 0.375
- convolution_bias: float32 [32], replicated, may hold values from -4 to 4
- readout: float32 [32], replicated, may hold values from -1 to 1
- targets: bfloat16 [64, 128, 2048], P('row', None, 'diag'), may hold values from -6 to 6
- block_order: int32 [64], replicated, may hold values from 0 to 63, each once
- band_reach: int32 [64], replicated, may hold values from 512 to 1919
Outputs:
- codes_grad: float32 [8192, 64], P(('row', 'diag'))
- conv_grad: float32 [9216], P(('row', 'diag'))
The draws below stay inside these ranges and needn't reach their ends.
All inputs are finite; a program needn't handle non-finite values.
Results may differ from the reference program's by a relative error of at most 0.0016.
Values may be sent and summed in bfloat16 or wider, within the bound.
No kernel may reach another device: no remote copies, remote signals or barrier semaphores. Data moves between devices by JAX's collectives and lax.ppermute only.
A program may use at most 256 MiB of HBM per device.

```python
import jax
import jax.numpy as jnp
from jax import lax

EMB = 256
C = 32
TILE_SIDE_BINS = 128
DILATION_STEP = 16
BAND_TILE_COUNT = 16
ROW_BLOCK_COUNT = 64
BINS = 8192


def place_ends(drawn, rng, smallest, high):
    spot = [jax.random.randint(jax.random.fold_in(rng, axis), (), 0, length) for axis, length in enumerate(drawn.shape)]
    main_axis = drawn.shape.index(max(drawn.shape))
    neighbour = spot[:main_axis] + [(spot[main_axis] + 1) % drawn.shape[main_axis]] + spot[main_axis + 1:]
    return drawn.at[tuple(spot)].set(smallest).at[tuple(neighbour)].set(high)


def block_levels(stream_key, extent, pieces, low, largest):
    def one(dim, blocks):
        steps = jax.random.uniform(jax.random.fold_in(jax.random.fold_in(stream_key, 6), dim), (blocks,), jnp.float32, low / len(pieces), largest / len(pieces))
        return jnp.repeat(jnp.exp(steps), extent[dim] // blocks).reshape((-1,) + (1,) * (len(extent) - dim - 1))

    factor_of = one(*pieces[0])
    for cut in pieces[1:]:
        factor_of = factor_of * one(*cut)
    return factor_of


def normal_values(key, extent, width, most, split=(), held_as=jnp.bfloat16):
    drawn = width * jax.random.normal(key, extent, jnp.float32)
    if split:
        drawn = drawn * block_levels(key, extent, split, -0.22, 0.18)
    return jnp.clip(drawn, -most, most).astype(held_as)


def setup_inputs(seed: int = 0) -> dict:
    keys = jax.random.split(jax.random.key(seed), 9)
    bins_x = normal_values(keys[0], (BINS, EMB), 1.0, 6.0, ((0, 128),))
    proj_weight = normal_values(keys[1], (EMB, 2 * C), EMB ** -0.5, 0.375)
    convolution_weight = normal_values(keys[2], (9, C, C), (9 * C) ** -0.5, 0.375)
    convolution_bias = normal_values(keys[3], (C,), 1.0, 4.0, (), jnp.float32)
    readout = normal_values(keys[4], (C,), C ** -0.5, 1.0, (), jnp.float32)
    targets = normal_values(keys[5], (ROW_BLOCK_COUNT, TILE_SIDE_BINS, BAND_TILE_COUNT * TILE_SIDE_BINS), 1.0, 6.0, ((0, 8), (2, 16)))
    block_order = jax.random.permutation(keys[6], ROW_BLOCK_COUNT).astype(jnp.int32)
    band_reach = place_ends(jax.random.randint(keys[7], (ROW_BLOCK_COUNT,), BAND_TILE_COUNT * TILE_SIDE_BINS // 4, BAND_TILE_COUNT * TILE_SIDE_BINS - TILE_SIDE_BINS), jax.random.fold_in(keys[7], 1), BAND_TILE_COUNT * TILE_SIDE_BINS // 4, (BAND_TILE_COUNT * TILE_SIDE_BINS - TILE_SIDE_BINS) - 1).astype(jnp.int32)
    return {"bins_x": bins_x, "proj_weight": proj_weight, "convolution_weight": convolution_weight, "convolution_bias": convolution_bias, "readout": readout, "targets": targets, "block_order": block_order, "band_reach": band_reach}


SQRT_HALF = 0.7071067811865476
INV_SQRT_TAU = 0.3989422804014327


def grid_cells(row_cell_ids, column_cell_ids, block_total):
    row_blocks = jnp.floor_divide(row_cell_ids, TILE_SIDE_BINS)[:, None]
    col_blocks = jnp.floor_divide(column_cell_ids, TILE_SIDE_BINS)[None, :]
    return (row_blocks >= 0) & (row_blocks < block_total) & (col_blocks >= row_blocks) & (col_blocks - row_blocks < BAND_TILE_COUNT) & (col_blocks < block_total)


def loss_cells(row_cell_ids, column_cell_ids, band_reach, block_total):
    in_grid = grid_cells(row_cell_ids, column_cell_ids, block_total)
    row_blocks = jnp.floor_divide(row_cell_ids, TILE_SIDE_BINS)
    labels = jnp.arange(block_total, dtype=jnp.int32)
    reach_rows = jnp.sum(jnp.where(row_blocks[:, None] == labels[None, :], band_reach[None, :], 0), axis=1)
    distance = column_cell_ids[None, :] - row_cell_ids[:, None]
    return in_grid & (distance >= 0) & (distance <= reach_rows[:, None])


def build_pair_maps(padded_codes, row_begin, column_begin, output_rows, output_columns, border_width, block_total):
    row_code_values = lax.dynamic_slice_in_dim(padded_codes, row_begin - border_width + 2 * DILATION_STEP, output_rows + 2 * border_width, 0).astype(jnp.float32)
    column_codes = lax.dynamic_slice_in_dim(padded_codes, column_begin - border_width + 2 * DILATION_STEP, output_columns + 2 * border_width, 0).astype(jnp.float32)
    row_cell_ids = row_begin - border_width + jnp.arange(output_rows + 2 * border_width, dtype=jnp.int32)
    column_cell_ids = column_begin - border_width + jnp.arange(output_columns + 2 * border_width, dtype=jnp.int32)
    u_rows = row_code_values[:, :C].T
    w_rows = row_code_values[:, C:].T
    u_cols = column_codes[:, :C].T
    w_cols = column_codes[:, C:].T
    pairwise_maps = u_rows[:, :, None] + u_cols[:, None, :] + w_rows[:, :, None] * w_cols[:, None, :]
    in_grid = grid_cells(row_cell_ids, column_cell_ids, block_total)
    return jnp.where(in_grid[None], pairwise_maps, 0.0).astype(jnp.bfloat16)


def convolution_forward(pairwise_maps, weights, convolution_bias, output_rows, output_columns):
    maps_float32 = pairwise_maps.astype(jnp.float32)
    weights32 = weights.astype(jnp.float32)
    summed = jnp.zeros((C, output_rows, output_columns), jnp.float32)
    for tap_index in range(9):
        kernel_tap_row = tap_index // 3
        kernel_tap_column = tap_index % 3
        displaced_maps = maps_float32[:, DILATION_STEP * kernel_tap_row:DILATION_STEP * kernel_tap_row + output_rows, DILATION_STEP * kernel_tap_column:DILATION_STEP * kernel_tap_column + output_columns]
        summed = summed + jnp.einsum('oc,cpq->opq', weights32[tap_index], displaced_maps, precision=lax.Precision.HIGHEST)
    return summed + convolution_bias[:, None, None]


def conv_transpose(grad_maps, weights, output_rows, output_columns):
    gradients_float32 = grad_maps.astype(jnp.float32)
    weights32 = weights.astype(jnp.float32)
    summed = jnp.zeros((C, output_rows, output_columns), jnp.float32)
    for tap_index in range(9):
        kernel_tap_row = tap_index // 3
        kernel_tap_column = tap_index % 3
        displaced_maps = gradients_float32[:, DILATION_STEP * (2 - kernel_tap_row):DILATION_STEP * (2 - kernel_tap_row) + output_rows, DILATION_STEP * (2 - kernel_tap_column):DILATION_STEP * (2 - kernel_tap_column) + output_columns]
        summed = summed + jnp.einsum('oc,opq->cpq', weights32[tap_index], displaced_maps, precision=lax.Precision.HIGHEST)
    return summed


def head_grads(convolution_output, target, mask, readout):
    normal_cdf = 0.5 * (1.0 + jax.scipy.special.erf(convolution_output * SQRT_HALF))
    density = jnp.exp(-0.5 * convolution_output * convolution_output) * INV_SQRT_TAU
    pred = jnp.sum(readout[:, None, None] * convolution_output * normal_cdf, axis=0)
    mismatch = jnp.where(mask, pred - target, 0.0) * (TILE_SIDE_BINS ** -0.5)
    return (readout[:, None, None] * mismatch[None] * (normal_cdf + convolution_output * density)).astype(jnp.bfloat16)


def accumulate(totals, gradient_extended, interior_maps, row_begin, column_begin, output_columns, weights, padded_codes, block_total):
    grads, conv_sum = totals
    local_gradients = gradient_extended[:, DILATION_STEP:DILATION_STEP + TILE_SIDE_BINS, DILATION_STEP:DILATION_STEP + output_columns].astype(jnp.float32)
    pair_grad = conv_transpose(gradient_extended, weights, TILE_SIDE_BINS, output_columns)
    row_cell_ids = row_begin + jnp.arange(TILE_SIDE_BINS, dtype=jnp.int32)
    column_cell_ids = column_begin + jnp.arange(output_columns, dtype=jnp.int32)
    pair_grad = jnp.where(grid_cells(row_cell_ids, column_cell_ids, block_total)[None], pair_grad, 0.0)
    row_code_values = lax.dynamic_slice_in_dim(padded_codes, row_begin + 2 * DILATION_STEP, TILE_SIDE_BINS, 0).astype(jnp.float32)
    column_codes = lax.dynamic_slice_in_dim(padded_codes, column_begin + 2 * DILATION_STEP, output_columns, 0).astype(jnp.float32)
    row_terms = jnp.concatenate([jnp.sum(pair_grad, axis=2).T, jnp.einsum('cpq,qc->pc', pair_grad, column_codes[:, C:], precision=lax.Precision.HIGHEST)], axis=1)
    col_terms = jnp.concatenate([jnp.sum(pair_grad, axis=1).T, jnp.einsum('cpq,pc->qc', pair_grad, row_code_values[:, C:], precision=lax.Precision.HIGHEST)], axis=1)
    grads = lax.dynamic_update_slice_in_dim(grads, lax.dynamic_slice_in_dim(grads, row_begin, TILE_SIDE_BINS, 0) + row_terms, row_begin, 0)
    grads = lax.dynamic_update_slice_in_dim(grads, lax.dynamic_slice_in_dim(grads, column_begin, output_columns, 0) + col_terms, column_begin, 0)
    maps_float32 = interior_maps.astype(jnp.float32)
    tap_terms = []
    for tap_index in range(9):
        kernel_tap_row = tap_index // 3
        kernel_tap_column = tap_index % 3
        displaced_maps = maps_float32[:, DILATION_STEP * kernel_tap_row:DILATION_STEP * kernel_tap_row + TILE_SIDE_BINS, DILATION_STEP * kernel_tap_column:DILATION_STEP * kernel_tap_column + output_columns]
        tap_terms.append(jnp.einsum('opq,cpq->oc', local_gradients, displaced_maps, precision=lax.Precision.HIGHEST))
    return grads, conv_sum + jnp.stack(tap_terms, axis=0)


def reference(bins_x, proj_weight, convolution_weight, convolution_bias, readout, targets, block_order, band_reach):
    code_rows = jnp.dot(bins_x, proj_weight, preferred_element_type=jnp.float32).astype(jnp.bfloat16)
    positions = jnp.arange(ROW_BLOCK_COUNT, dtype=jnp.int32)
    inverse = jnp.sum(jnp.where(block_order[:, None] == positions[None, :], positions[:, None], 0), axis=0).astype(jnp.int32)
    binned_codes = jnp.take(code_rows.reshape(ROW_BLOCK_COUNT, TILE_SIDE_BINS, 2 * C), inverse, axis=0).reshape(BINS, 2 * C)
    padded_codes = jnp.pad(binned_codes, ((2 * DILATION_STEP, BAND_TILE_COUNT * TILE_SIDE_BINS + 2 * DILATION_STEP), (0, 0)))
    strip_columns = BAND_TILE_COUNT * TILE_SIDE_BINS

    def step(totals, block_index):
        row_begin = (block_index * TILE_SIDE_BINS).astype(jnp.int32)
        column_begin = row_begin
        pairwise_maps = build_pair_maps(padded_codes, row_begin, column_begin, TILE_SIDE_BINS, strip_columns, 2 * DILATION_STEP, ROW_BLOCK_COUNT)
        convolution_output = convolution_forward(pairwise_maps, convolution_weight, convolution_bias, TILE_SIDE_BINS + 2 * DILATION_STEP, strip_columns + 2 * DILATION_STEP)
        row_cell_ids = row_begin - DILATION_STEP + jnp.arange(TILE_SIDE_BINS + 2 * DILATION_STEP, dtype=jnp.int32)
        column_cell_ids = column_begin - DILATION_STEP + jnp.arange(strip_columns + 2 * DILATION_STEP, dtype=jnp.int32)
        in_grid = grid_cells(row_cell_ids, column_cell_ids, ROW_BLOCK_COUNT)
        row_blocks = jnp.clip(jnp.floor_divide(row_cell_ids, TILE_SIDE_BINS), 0, ROW_BLOCK_COUNT - 1).astype(jnp.int32)
        local_rows = jnp.clip(row_cell_ids - row_blocks * TILE_SIDE_BINS, 0, TILE_SIDE_BINS - 1).astype(jnp.int32)
        local_cols = jnp.clip(column_cell_ids[None, :] - (row_blocks * TILE_SIDE_BINS)[:, None], 0, strip_columns - 1).astype(jnp.int32)
        looked = targets[row_blocks[:, None], local_rows[:, None], local_cols].astype(jnp.float32)
        target = jnp.where(in_grid, looked, 0.0)
        gradient_extended = head_grads(convolution_output, target, loss_cells(row_cell_ids, column_cell_ids, band_reach, ROW_BLOCK_COUNT), readout)
        interior_maps = pairwise_maps[:, DILATION_STEP:DILATION_STEP + TILE_SIDE_BINS + 2 * DILATION_STEP, DILATION_STEP:DILATION_STEP + strip_columns + 2 * DILATION_STEP]
        return accumulate(totals, gradient_extended, interior_maps, row_begin, column_begin, strip_columns, convolution_weight, padded_codes, ROW_BLOCK_COUNT), None

    start = (jnp.zeros((BINS + BAND_TILE_COUNT * TILE_SIDE_BINS, 2 * C), jnp.float32), jnp.zeros((9, C, C), jnp.float32))
    (grads, conv_sum), _ = lax.scan(step, start, jnp.arange(ROW_BLOCK_COUNT, dtype=jnp.int32))
    grads_bin = grads[:BINS]
    codes_grad = jnp.take(grads_bin.reshape(ROW_BLOCK_COUNT, TILE_SIDE_BINS, 2 * C), block_order, axis=0).reshape(BINS, 2 * C)
    conv_grad = (conv_sum / ROW_BLOCK_COUNT).reshape(-1)
    return codes_grad, conv_grad
```

```python
import functools

import jax
import jax.numpy as jnp
from jax import lax
from jax.experimental import pallas as pl
from jax.experimental.pallas import tpu as pltpu
from jax.sharding import PartitionSpec as P

C = 32
TILE = 128
STEP = 16
BAND = 16
GROUPS = TILE // STEP
PAIRS = GROUPS // 2
SLABS = GROUPS + 2
SPAN = TILE + 2 * STEP
PLANE = PAIRS * STEP
ROWS = STEP * PLANE
CHUNK = 512

SQRT_HALF = 0.7071067811865476
INV_SQRT_TAU = 0.3989422804014327
BF = jnp.bfloat16
F32 = jnp.float32


def dot(a, b, dims=(((1,), (0,)), ((), ()))):
    return lax.dot_general(a, b, dims, preferred_element_type=F32)


def lane_fold(x):
    x = x + pltpu.roll(x, 64, 1)
    return x + pltpu.roll(x, 32, 1)


def tile_kernel(
    blocks,
    tiles,
    s_ref,
    row_prev,
    row_here,
    row_next,
    col_prev,
    col_here,
    col_next,
    tgt_ref,
    wf_ref,
    wb_ref,
    spread_ref,
    ones_ref,
    place_ref,
    vec_ref,
    grads_ref,
    taps_ref,
    u_row,
    w_row,
    uq_s,
    wq_s,
    mask_s,
    dist_s,
    x_s,
    r0_s,
    r1_s,
    c0_s,
    c1_s,
    acc_s,
    row_acc,
    col_acc,
):
    t = pl.program_id(0)
    a = s_ref[2 * blocks] * tiles + t
    d = s_ref[2 * blocks + 1]
    b = a + d
    reach = s_ref[blocks + a]

    @pl.when(t == 0)
    def _():
        acc_s[...] = jnp.zeros_like(acc_s)
        row_acc[...] = jnp.zeros_like(row_acc)
        col_acc[...] = jnp.zeros_like(col_acc)
        line = lax.broadcasted_iota(jnp.int32, (ROWS, 256), 0)
        lane = lax.broadcasted_iota(jnp.int32, (ROWS, 256), 1)
        r = line // PLANE
        jp = (line % PLANE) // STEP
        s = line % STEP
        ii = lane // 64
        jj = (lane // 32) % 2
        dist_s[...] = 32 * jp + s - r + 16 * (jj - ii)

    def codes(prev, here, after):
        left, right = spread_ref[0], spread_ref[1]
        return jnp.concatenate(
            [
                dot(prev[0], right),
                dot(here[0], left),
                dot(here[0], right),
                dot(here[1], left),
                dot(here[1], right),
                dot(after[0], left),
            ],
            axis=0,
        )

    row_codes = codes(row_prev, row_here, row_next)
    u_row[...] = row_codes[:, :128]
    w_row[...] = row_codes[:, 128:]
    col_codes = codes(col_prev, col_here, col_next).reshape(SLABS, STEP, 256)
    group = lax.broadcasted_iota(jnp.int32, (STEP, 256), 1) // C % 4
    for jp in range(PAIRS):
        window = col_codes[2 * jp]
        for g in range(1, 4):
            window = jnp.where(group == g, col_codes[2 * jp + g], window)
        uq_s[jp * STEP : (jp + 1) * STEP, :] = window[:, :128]
        wq_s[jp * STEP : (jp + 1) * STEP, :] = window[:, 128:]

    line = lax.broadcasted_iota(jnp.int32, (PLANE, 128), 0)
    lane = lax.broadcasted_iota(jnp.int32, (PLANE, 128), 1)
    at_left = (line < STEP) & (lane < C)
    at_right = (line >= PLANE - STEP) & (lane >= 3 * C)
    for k in range(3):
        ar = a - 1 + k

        def inside(cb):
            ok = (ar >= 0) & (ar < blocks) & (cb >= ar) & (cb - ar < BAND) & (cb < blocks)
            return jnp.where(ok, 1.0, 0.0).astype(F32)

        mask_s[k] = jnp.where(
            at_left, inside(b - 1), jnp.where(at_right, inside(b + 1), inside(b))
        )

    uq = uq_s[...]
    wq = wq_s[...]

    def kind(i):
        return 0 if i == 0 else (2 if i == SLABS - 1 else 1)

    def make_maps(r, carry):
        for i in range(SLABS):
            u = u_row[pl.ds(i * STEP + r, 1), :]
            w = w_row[pl.ds(i * STEP + r, 1), :]
            value = ((u + uq) + w * wq) * mask_s[kind(i)]
            x_s[i, pl.ds(pl.multiple_of(r * PLANE, PLANE), PLANE), :] = value.astype(BF)
        return carry

    lax.fori_loop(0, STEP, make_maps, 0)

    c0_s[...] = jnp.zeros_like(c0_s)
    c1_s[...] = jnp.zeros_like(c1_s)
    bias = vec_ref[0:1, :]
    read = vec_ref[1:2, :]
    read_density = read * INV_SQRT_TAU
    planes = CHUNK // PLANE

    def step(ch, carry):
        r0 = ch * planes
        at = pl.multiple_of(ch * CHUNK, CHUNK)
        rows = pl.ds(at, CHUNK)
        grads = []
        for ig in range(2):
            maps = jnp.concatenate([x_s[4 * ig + i, rows, :] for i in range(6)], axis=1)
            v = dot(maps, wf_ref[...]) + bias
            cdf = 0.5 * (1.0 + lax.erf(v * SQRT_HALF))
            density = jnp.exp(-0.5 * v * v)
            read_cdf = read * cdf
            g = v * read_cdf
            high = g.astype(BF)
            low = (g - high.astype(F32)).astype(BF)
            pred = dot(high, ones_ref[...]) + dot(low, ones_ref[...])
            target = dot(tgt_ref[0, rows, :], place_ref[ig])
            lowest = 64 * ig - TILE * d
            highest = jnp.where(b < blocks, reach + lowest, -100000)
            dist = dist_s[rows, :]
            keep = (dist >= lowest) & (dist <= highest)
            err = jnp.where(keep, pred - target, 0.0) * TILE ** (-0.5)
            grad = (err * (read_cdf + read_density * (v * density))).astype(BF)
            grads.append(grad)
            acc_s[...] += dot(grad, maps, (((0,), (0,)), ((), ())))
        for k in range(SLABS // 2):
            total = None
            for ig in range(2):
                slot = k - 2 * ig
                if 0 <= slot < 3:
                    part = dot(grads[ig], wb_ref[:, 256 * slot : 256 * (slot + 1)])
                    total = part if total is None else total + part
            for half in range(2):
                i = 2 * k + half
                dx = total[:, 128 * half : 128 * (half + 1)].reshape(planes, PLANE, 128)
                dx = dx * mask_s[kind(i)][None]
                dxw = dx * wq_s[...][None]
                for rr in range(planes):
                    p = i * STEP + r0 + rr
                    r0_s[p] = jnp.sum(dx[rr].reshape(PLANE // 8, 8, 128), axis=0)
                    r1_s[p] = jnp.sum(dxw[rr].reshape(PLANE // 8, 8, 128), axis=0)
                    c0_s[...] += dx[rr]
                    c1_s[...] += dx[rr] * w_row[pl.ds(p, 1), :]
        return carry

    lax.fori_loop(0, ROWS // CHUNK, step, 0)

    lanes = lax.broadcasted_iota(jnp.int32, (SPAN, 128), 1)
    even = lanes // C % 2 == 0
    row_terms = jnp.where(
        even,
        lane_fold(jnp.sum(r0_s[...], axis=1)),
        lane_fold(jnp.sum(r1_s[...], axis=1)),
    )
    here = pl.ds(pl.multiple_of(t * TILE, TILE), SPAN)
    row_acc[here, :] += row_terms

    group = lax.broadcasted_iota(jnp.int32, (STEP, 128), 1) // C

    def unwind(ref):
        parts = []
        for m in range(PAIRS + 1):
            for odd in range(2):
                value = jnp.zeros((STEP, 128), F32)
                if m < PAIRS:
                    value = jnp.where(group == odd, ref[m * STEP : (m + 1) * STEP, :], value)
                if m > 0:
                    value = jnp.where(group == 2 + odd, ref[(m - 1) * STEP : m * STEP, :], value)
                parts.append(value)
        return lane_fold(jnp.concatenate(parts, axis=0))

    col_acc[here, :] += jnp.where(even, unwind(c0_s), unwind(c1_s))

    @pl.when(t == tiles - 1)
    def _():
        grads_ref[...] = jnp.zeros_like(grads_ref)
        first = s_ref[2 * blocks] * tiles
        low_half = lax.broadcasted_iota(jnp.int32, (32, 128), 1) < 64

        def put(acc_ref, base, k, begin, count):
            n = base + k

            @pl.when((n >= 0) & (n < blocks))
            def _():
                slot = s_ref[n]
                for h in range(2):
                    top = acc_ref[pl.ds(begin + 64 * h, 32), :]
                    bottom = acc_ref[pl.ds(begin + 64 * h + 32, 32), :]
                    grads_ref[2 * slot + h] += jnp.where(low_half, top, bottom)

        for acc_ref, base in ((row_acc, first), (col_acc, first + d)):
            for k in range(tiles):
                put(acc_ref, base, k, STEP + k * TILE, TILE)

            @pl.when((base > 0) & (base <= blocks))
            def _():
                slot = s_ref[jnp.clip(base - 1, 0, blocks - 1)]
                grads_ref[2 * slot + 1, pl.ds(16, 16), :] += jnp.where(
                    low_half[:16], 0.0, acc_ref[0:STEP, :]
                )

            @pl.when(base + tiles < blocks)
            def _():
                slot = s_ref[jnp.minimum(base + tiles, blocks - 1)]
                grads_ref[2 * slot, pl.ds(0, 16), :] += jnp.where(
                    low_half[:16], acc_ref[STEP + tiles * TILE : 2 * STEP + tiles * TILE, :], 0.0
                )

        for ty in range(3):
            total = acc_s[0:64, 128 * ty : 128 * (ty + 1)]
            for ii in range(1, 4):
                total = total + acc_s[
                    64 * ii : 64 * (ii + 1), 128 * (ii + ty) : 128 * (ii + ty + 1)
                ]
            taps_ref[ty] = total[:C] + pltpu.roll(total[C:], 96, 1)


def run_tiles(scalars, code_chunks, tgt, wf, wb, vec, blocks, tiles):
    lane = jnp.arange(256, dtype=jnp.int32)
    source = lane // 128 * C + lane % C
    depth = jnp.arange(128, dtype=jnp.int32)
    spread = jnp.stack(
        [depth[:, None] == source[None, :], depth[:, None] == 64 + source[None, :]]
    ).astype(BF)
    ones = (lane[:, None] // C == lane[None, :] // C).astype(BF)
    sixteen = jnp.arange(16, dtype=jnp.int32)
    place = jnp.stack(
        [sixteen[:, None] == 8 * ig + lane[None, :] // C for ig in range(2)]
    ).astype(BF)

    def chunk_spec(offset, column, edge):
        def index(t, s):
            n = s[2 * blocks] * tiles + t + offset
            if column:
                n = n + s[2 * blocks + 1]
            n = s[jnp.clip(n, 0, blocks - 1)]
            if edge < 0:
                return (2 * n + 1, 1, 0)
            if edge > 0:
                return (2 * n, 0, 0)
            return (n, 0, 0)

        return pl.BlockSpec((1, STEP, 128) if edge else (2, 32, 128), index)

    def whole(x):
        zeros = (0,) * x.ndim
        return pl.BlockSpec(x.shape, lambda t, s: zeros)

    grid_spec = pltpu.PrefetchScalarGridSpec(
        num_scalar_prefetch=1,
        grid=(tiles,),
        in_specs=[
            chunk_spec(-1, False, -1),
            chunk_spec(0, False, 0),
            chunk_spec(1, False, 1),
            chunk_spec(-1, True, -1),
            chunk_spec(0, True, 0),
            chunk_spec(1, True, 1),
            pl.BlockSpec((1, ROWS, 16), lambda t, s: (t, 0, 0)),
            whole(wf),
            whole(wb),
            whole(spread),
            whole(ones),
            whole(place),
            whole(vec),
        ],
        out_specs=[
            pl.BlockSpec((2 * blocks, 32, 128), lambda t, s: (0, 0, 0)),
            pl.BlockSpec((3, C, 128), lambda t, s: (0, 0, 0)),
        ],
        scratch_shapes=[
            pltpu.VMEM((SPAN, 128), F32),
            pltpu.VMEM((SPAN, 128), F32),
            pltpu.VMEM((PLANE, 128), F32),
            pltpu.VMEM((PLANE, 128), F32),
            pltpu.VMEM((3, PLANE, 128), F32),
            pltpu.VMEM((ROWS, 256), jnp.int32),
            pltpu.VMEM((SLABS, ROWS, 128), BF),
            pltpu.VMEM((SPAN, 8, 128), F32),
            pltpu.VMEM((SPAN, 8, 128), F32),
            pltpu.VMEM((PLANE, 128), F32),
            pltpu.VMEM((PLANE, 128), F32),
            pltpu.VMEM((256, 768), F32),
            pltpu.VMEM((tiles * TILE + 2 * STEP, 128), F32),
            pltpu.VMEM((tiles * TILE + 2 * STEP, 128), F32),
        ],
    )
    return pl.pallas_call(
        functools.partial(tile_kernel, blocks, tiles),
        grid_spec=grid_spec,
        out_shape=[
            jax.ShapeDtypeStruct((2 * blocks, 32, 128), F32),
            jax.ShapeDtypeStruct((3, C, 128), F32),
        ],
        compiler_params=pltpu.CompilerParams(
            dimension_semantics=("arbitrary",), vmem_limit_bytes=48 * 1024 * 1024
        ),
    )(
        scalars,
        code_chunks,
        code_chunks,
        code_chunks,
        code_chunks,
        code_chunks,
        code_chunks,
        tgt,
        wf,
        wb,
        spread,
        ones,
        place,
        vec,
    )


def per_device(
    bins_x,
    proj_weight,
    convolution_weight,
    convolution_bias,
    readout,
    targets,
    block_order,
    band_reach,
):
    tiles = targets.shape[0]
    blocks = block_order.shape[0]
    axes = ("row", "diag")
    code_local = dot(bins_x, proj_weight).astype(BF)
    packed = jnp.concatenate([code_local[:32], code_local[32:]], axis=1)
    code_chunks = lax.all_to_all(
        jnp.broadcast_to(packed[None], (2 * blocks, 32, 128)), axes, 0, 0, tiled=True
    )
    positions = jnp.arange(blocks, dtype=jnp.int32)
    inverse = jnp.sum(
        jnp.where(block_order[:, None] == positions[None, :], positions[:, None], 0), axis=0
    )
    scalars = jnp.concatenate(
        [
            inverse,
            band_reach,
            jnp.stack([lax.axis_index("row"), lax.axis_index("diag")]).astype(jnp.int32),
        ]
    )
    tgt = (
        targets.reshape(tiles, GROUPS, STEP, PAIRS, 2, STEP)
        .transpose(0, 2, 3, 5, 1, 4)
        .reshape(tiles, ROWS, 2 * GROUPS)
    )
    taps = convolution_weight.reshape(3, 3, C, C).transpose(0, 1, 3, 2)
    wf = jnp.stack(
        [
            jnp.pad(taps, ((ii, 3 - ii), (jj, 1 - jj), (0, 0), (0, 0)))
            for ii in range(4)
            for jj in range(2)
        ],
        axis=3,
    ).reshape(768, 256)
    wb = wf.T
    vec = jnp.stack([jnp.tile(convolution_bias, 8), jnp.tile(readout, 8)])
    grads, tap_sums = run_tiles(scalars, code_chunks, tgt, wf, wb, vec, blocks, tiles)
    tap_flat = (
        tap_sums[:, :, : 3 * C].reshape(3, C, 3, C).transpose(0, 2, 1, 3).reshape(2 * blocks, -1)
        / blocks
    )
    owned = tap_flat.shape[1]
    tap_rows = jnp.pad(tap_flat, ((0, 0), (0, 1024 - owned))).reshape(2 * blocks, 8, 128)
    terms = jnp.concatenate([grads.astype(BF), tap_rows.astype(BF)], axis=1)
    received = lax.all_to_all(terms, axes, 0, 0, tiled=True)
    mine = jnp.sum(received.astype(F32), axis=0)
    codes_grad = jnp.concatenate([mine[:32, :64], mine[:32, 64:]], axis=0)
    conv_grad = mine[32, :owned]
    return (codes_grad, conv_grad)


def solution(mesh):
    in_specs = (P(("row", "diag"), None), P(), P(), P(), P(), P("row", None, "diag"), P(), P())
    out_specs = (P(("row", "diag"), None), P(("row", "diag")))
    return jax.shard_map(
        per_device, mesh=mesh, in_specs=in_specs, out_specs=out_specs, check_vma=False
    )
```

```python
import functools

import jax
import jax.numpy as jnp
from jax import lax
from jax.experimental import pallas as pl
from jax.experimental.pallas import tpu as pltpu
from jax.sharding import PartitionSpec as P

C = 32
TILE = 128
STEP = 16
BAND = 16
PAIRS = TILE // (2 * STEP)
SLABS = TILE // STEP + 2
SPAN = TILE + 2 * STEP
PLANE = PAIRS * STEP
ROWS = STEP * PLANE
CHUNK = 512
MPIECE = 512

SQRT_HALF = 0.7071067811865476
INV_SQRT_TAU = 0.3989422804014327
BF = jnp.bfloat16
F32 = jnp.float32


def dot(a, b, dims=(((1,), (0,)), ((), ()))):
    return lax.dot_general(a, b, dims, preferred_element_type=F32)


def lane_fold(x):
    x = x + pltpu.roll(x, 64, 1)
    return x + pltpu.roll(x, 32, 1)


def weave(*streams):
    streams = [list(x) for x in streams if x]
    order = sorted(
        ((n + 0.5) / len(x), m, n) for m, x in enumerate(streams) for n in range(len(x))
    )
    for _, m, n in order:
        streams[m][n]()


def tile_kernel(
    blocks,
    tiles,
    s_ref,
    row_prev,
    row_here,
    row_next,
    col_prev,
    col_here,
    col_next,
    tgt_ref,
    wf_ref,
    wb_ref,
    spread_ref,
    place_ref,
    vec_ref,
    grads_ref,
    taps_ref,
    u_row,
    w_row,
    uq_s,
    wq_s,
    mask_s,
    dist_s,
    tgt_s,
    x_s,
    r0_s,
    r1_s,
    c0_s,
    c1_s,
    acc_s,
    row_acc,
    col_acc,
):
    g = pl.program_id(0)
    new = g % 2
    old = 1 - new
    d = s_ref[2 * blocks + 1]
    first = s_ref[2 * blocks] * tiles

    @pl.when(g == 0)
    def _():
        acc_s[...] = jnp.zeros_like(acc_s)
        row_acc[...] = jnp.zeros_like(row_acc)
        col_acc[...] = jnp.zeros_like(col_acc)
        line = lax.broadcasted_iota(jnp.int32, (ROWS, 256), 0)
        lane = lax.broadcasted_iota(jnp.int32, (ROWS, 256), 1)
        r = line // PLANE
        jp = (line % PLANE) // STEP
        s = line % STEP
        ii = lane // 64
        jj = (lane // 32) % 2
        dist_s[...] = 32 * jp + s - r + 16 * (jj - ii)

    def codes(prev, here, after):
        left, right = spread_ref[0], spread_ref[1]
        return jnp.concatenate(
            [
                dot(prev[0], right),
                dot(here[0], left),
                dot(here[0], right),
                dot(here[1], left),
                dot(here[1], right),
                dot(after[0], left),
            ],
            axis=0,
        )

    def kind(i):
        return 0 if i == 0 else (2 if i == SLABS - 1 else 1)

    row_codes = codes(row_prev, row_here, row_next)
    u_row[...] = row_codes[:, :128]
    w_row[new] = row_codes[:, 128:]
    col_codes = codes(col_prev, col_here, col_next).reshape(SLABS, STEP, 256)
    group = lax.broadcasted_iota(jnp.int32, (STEP, 256), 1) // C % 4
    for jp in range(PAIRS):
        window = col_codes[2 * jp]
        for m in range(1, 4):
            window = jnp.where(group == m, col_codes[2 * jp + m], window)
        uq_s[jp * STEP : (jp + 1) * STEP, :] = window[:, :128]
        wq_s[new, jp * STEP : (jp + 1) * STEP, :] = window[:, 128:]
    line = lax.broadcasted_iota(jnp.int32, (PLANE, 128), 0)
    lane = lax.broadcasted_iota(jnp.int32, (PLANE, 128), 1)
    at_left = (line < STEP) & (lane < C)
    at_right = (line >= PLANE - STEP) & (lane >= 3 * C)
    for k in range(3):
        ar = first + g - 1 + k

        def inside(cb):
            ok = (ar >= 0) & (ar < blocks) & (cb >= ar) & (cb - ar < BAND) & (cb < blocks)
            return jnp.where(ok, 1.0, 0.0).astype(F32)

        bg = first + g + d
        mask_s[new, k] = jnp.where(
            at_left, inside(bg - 1), jnp.where(at_right, inside(bg + 1), inside(bg))
        )

    def edged(value, which, k):
        mask = mask_s.at[which, k]
        if k != 1:
            return value * mask[...]
        return jnp.concatenate(
            [
                value[:STEP] * mask[:STEP, :],
                value[STEP : PLANE - STEP],
                value[PLANE - STEP :] * mask[PLANE - STEP :, :],
            ],
            axis=0,
        )

    def make_map(i, r):
        u = u_row[pl.ds(i * STEP + r, 1), :]
        w = w_row[new, pl.ds(i * STEP + r, 1), :]
        value = edged((u + uq_s[...]) + w * wq_s[new], new, kind(i))
        x_s[new, i, pl.ds(r * PLANE, PLANE), :] = value.astype(BF)

    def make_maps(r, carry):
        for i in range(SLABS):
            make_map(i, r)
        return carry

    @pl.when(g == 0)
    def _():
        lax.fori_loop(0, STEP, make_maps, 0)

    bias = vec_ref[0:1, :]
    read = vec_ref[1:2, :]
    half_read = 0.5 * read
    read_density = read * INV_SQRT_TAU
    planes = CHUNK // PLANE

    def tile(t):
        a = first + t
        b = a + d
        reach = s_ref[blocks + a]
        c0_s[...] = jnp.zeros_like(c0_s)
        c1_s[...] = jnp.zeros_like(c1_s)

        turned = tgt_ref[0].astype(F32).T.reshape(PAIRS, 2, STEP, TILE)
        sides = [turned[:, jj].reshape(PLANE, TILE) for jj in range(2)]

        def make_target(r):
            for jj in range(2):
                value = sides[jj] if r == 0 else pltpu.roll(sides[jj], TILE - r, 1)
                tgt_s[r * PLANE : (r + 1) * PLANE, TILE * jj : TILE * (jj + 1)] = value.astype(BF)

        n = ROWS // CHUNK
        todo = [(ch, ig) for ch in range(n) for ig in range(2)]
        vs, parts, grads = {}, {}, {}

        def maps(ch, ig, begin=0, count=CHUNK):
            rows = pl.ds(ch * CHUNK + begin, count)
            return jnp.concatenate([x_s[old, 4 * ig + i, rows, :] for i in range(6)], axis=1)

        def forward(m):
            ch, ig = todo[m]
            def piece(begin):
                vs[m, begin] = dot(maps(ch, ig, begin, MPIECE), wf_ref[...])

            return [functools.partial(piece, x) for x in range(0, CHUNK, MPIECE)]

        def slope(m):
            def piece(begin):
                base = begin // MPIECE * MPIECE
                v = vs[m, base][begin - base : begin - base + PLANE] + bias
                x = v * SQRT_HALF
                read_cdf = half_read * lax.erf(x) + half_read
                value = v * read_cdf
                high = value.astype(BF)
                low = (value - high.astype(F32)).astype(BF)
                parts[m, begin] = (
                    high,
                    low,
                    read_cdf + (read_density * v) * jnp.exp(-(x * x)),
                )

            return [functools.partial(piece, x) for x in range(0, CHUNK, PLANE)]

        def error(m):
            ch, ig = todo[m]
            lowest = 64 * ig - TILE * d
            highest = jnp.where(b < blocks, reach + lowest, -100000)
            out = {}

            def predict(base):
                pieces = [parts[m, base + x] for x in range(0, MPIECE, PLANE)]
                terms = jnp.concatenate(
                    [
                        jnp.concatenate([x[0] for x in pieces], axis=0),
                        jnp.concatenate([x[1] for x in pieces], axis=0),
                        tgt_s[pl.ds(ch * CHUNK + base, MPIECE), :],
                    ],
                    axis=1,
                )
                out[base] = dot(terms, place_ref[ig])

            def piece(begin):
                base = begin // MPIECE * MPIECE
                dist = dist_s[pl.ds(ch * CHUNK + begin, PLANE), :]
                keep = (dist >= lowest) & (dist <= highest)
                miss = out[base][begin - base : begin - base + PLANE]
                err = jnp.where(keep, miss, 0.0) * TILE ** (-0.5)
                grads[m, begin] = (err * parts[m, begin][2]).astype(BF)

            todo_list = []
            for base in range(0, CHUNK, MPIECE):
                todo_list.append(functools.partial(predict, base))
                if base:
                    todo_list += [
                        functools.partial(piece, x) for x in range(base - MPIECE, base, PLANE)
                    ]
            todo_list += [
                functools.partial(piece, x) for x in range(CHUNK - MPIECE, CHUNK, PLANE)
            ]
            return todo_list

        def grad_of(m):
            return jnp.concatenate([grads[m, x] for x in range(0, CHUNK, PLANE)], axis=0)

        def taps(m):
            ch, ig = todo[m]

            def piece(k):
                rows = pl.ds(ch * CHUNK, CHUNK)
                two = jnp.concatenate(
                    [x_s[old, 4 * ig + 2 * k + i, rows, :] for i in range(2)], axis=1
                )
                acc_s[:, 256 * k : 256 * (k + 1)] += dot(
                    grad_of(m), two, (((0,), (0,)), ((), ()))
                )

            return [functools.partial(piece, k) for k in range(3)]

        def back(m):
            ch, _ = todo[m]
            totals = {}

            def product(k):
                total = None
                for ig in range(2):
                    slot = k - 2 * ig
                    if 0 <= slot < 3:
                        part = dot(grad_of(m - 1 + ig), wb_ref[:, 256 * slot : 256 * (slot + 1)])
                        total = part if total is None else total + part
                totals[k] = total

            def piece(k, half, rr):
                i = 2 * k + half
                p = i * STEP + ch * planes + rr
                dx = totals[k][rr * PLANE : (rr + 1) * PLANE, 128 * half : 128 * (half + 1)]
                dx = edged(dx, old, kind(i))
                c0_s[...] += dx
                c1_s[...] += dx * w_row[old, p : p + 1, :]
                r0_s[p] = jnp.sum(dx.reshape(PLANE // 8, 8, 128), axis=0)
                r1_s[p] = jnp.sum((dx * wq_s[old]).reshape(PLANE // 8, 8, 128), axis=0)

            out = []
            for k in range(SLABS // 2):
                out.append(functools.partial(product, k))
                if k:
                    out += [
                        functools.partial(piece, k - 1, half, rr)
                        for half in range(2)
                        for rr in range(planes)
                    ]
            out += [
                functools.partial(piece, SLABS // 2 - 1, half, rr)
                for half in range(2)
                for rr in range(planes)
            ]
            return out

        targets = [functools.partial(make_target, r) for r in range(STEP)]
        fresh = [functools.partial(make_map, i, r) for r in range(STEP) for i in range(SLABS)]
        units = len(todo)
        steps = units + 3
        for m in range(steps):
            share = fresh[len(fresh) * m // steps : len(fresh) * (m + 1) // steps]
            tgt_now = targets[STEP * m // 2 : STEP * (m + 1) // 2] if m < 2 else []
            weave(
                forward(m) if m < units else [],
                slope(m - 1) if 0 <= m - 1 < units else [],
                error(m - 2) if 0 <= m - 2 < units else [],
                taps(m - 3) if m >= 3 else [],
                back(m - 3) if m >= 3 and (m - 3) % 2 == 1 else [],
                share,
                tgt_now,
            )

        lanes = lax.broadcasted_iota(jnp.int32, (SPAN, 128), 1)
        even = lanes // C % 2 == 0
        row_terms = jnp.where(
            even,
            lane_fold(jnp.sum(r0_s[...], axis=1)),
            lane_fold(jnp.sum(r1_s[...], axis=1)),
        )
        here = pl.ds(pl.multiple_of(t * TILE, TILE), SPAN)
        row_acc[here, :] += row_terms

        group = lax.broadcasted_iota(jnp.int32, (STEP, 128), 1) // C

        def unwind(ref):
            pieces = []
            for m in range(PAIRS + 1):
                for odd in range(2):
                    value = jnp.zeros((STEP, 128), F32)
                    if m < PAIRS:
                        value = jnp.where(group == odd, ref[m * STEP : (m + 1) * STEP, :], value)
                    if m > 0:
                        value = jnp.where(
                            group == 2 + odd, ref[(m - 1) * STEP : m * STEP, :], value
                        )
                    pieces.append(value)
            return lane_fold(jnp.concatenate(pieces, axis=0))

        col_acc[here, :] += jnp.where(even, unwind(c0_s), unwind(c1_s))

    @pl.when(g > 0)
    def _():
        tile(g - 1)

    @pl.when(g == tiles)
    def _():
        grads_ref[...] = jnp.zeros_like(grads_ref)
        low_half = lax.broadcasted_iota(jnp.int32, (32, 128), 1) < 64

        def put(acc_ref, base, k, begin, count):
            n = base + k

            @pl.when((n >= 0) & (n < blocks))
            def _():
                slot = s_ref[n]
                for h in range(2):
                    top = acc_ref[pl.ds(begin + 64 * h, 32), :]
                    bottom = acc_ref[pl.ds(begin + 64 * h + 32, 32), :]
                    grads_ref[2 * slot + h] += jnp.where(low_half, top, bottom)

        for acc_ref, base in ((row_acc, first), (col_acc, first + d)):
            for k in range(tiles):
                put(acc_ref, base, k, STEP + k * TILE, TILE)

            @pl.when((base > 0) & (base <= blocks))
            def _():
                slot = s_ref[jnp.clip(base - 1, 0, blocks - 1)]
                grads_ref[2 * slot + 1, pl.ds(16, 16), :] += jnp.where(
                    low_half[:16], 0.0, acc_ref[0:STEP, :]
                )

            @pl.when(base + tiles < blocks)
            def _():
                slot = s_ref[jnp.minimum(base + tiles, blocks - 1)]
                grads_ref[2 * slot, pl.ds(0, 16), :] += jnp.where(
                    low_half[:16], acc_ref[STEP + tiles * TILE : 2 * STEP + tiles * TILE, :], 0.0
                )

        for ty in range(3):
            total = acc_s[0:64, 128 * ty : 128 * (ty + 1)]
            for ii in range(1, 4):
                total = total + acc_s[
                    64 * ii : 64 * (ii + 1), 128 * (ii + ty) : 128 * (ii + ty + 1)
                ]
            taps_ref[ty] = total[:C] + pltpu.roll(total[C:], 96, 1)


def run_tiles(scalars, code_chunks, targets, wf, wb, vec, blocks, tiles):
    lane = jnp.arange(256, dtype=jnp.int32)
    source = lane // 128 * C + lane % C
    depth = jnp.arange(128, dtype=jnp.int32)
    spread = jnp.stack(
        [depth[:, None] == source[None, :], depth[:, None] == 64 + source[None, :]]
    ).astype(BF)
    ones = lane[:, None] // C == lane[None, :] // C
    place = jnp.stack(
        [
            jnp.concatenate(
                [ones.astype(BF), ones.astype(BF)]
                + [
                    -(
                        (depth[:, None] == 16 * (4 * ig + lane[None, :] // 64))
                        & (lane[None, :] // C % 2 == jj)
                    ).astype(BF)
                    for jj in range(2)
                ],
                axis=0,
            )
            for ig in range(2)
        ]
    )

    def chunk_spec(offset, column, edge):
        def index(t, s):
            n = s[2 * blocks] * tiles + t + offset
            if column:
                n = n + s[2 * blocks + 1]
            n = s[jnp.clip(n, 0, blocks - 1)]
            if edge < 0:
                return (2 * n + 1, 1, 0)
            if edge > 0:
                return (2 * n, 0, 0)
            return (n, 0, 0)

        return pl.BlockSpec((1, STEP, 128) if edge else (2, 32, 128), index)

    def whole(x):
        zeros = (0,) * x.ndim
        return pl.BlockSpec(x.shape, lambda t, s: zeros)

    grid_spec = pltpu.PrefetchScalarGridSpec(
        num_scalar_prefetch=1,
        grid=(tiles + 1,),
        in_specs=[
            chunk_spec(-1, False, -1),
            chunk_spec(0, False, 0),
            chunk_spec(1, False, 1),
            chunk_spec(-1, True, -1),
            chunk_spec(0, True, 0),
            chunk_spec(1, True, 1),
            pl.BlockSpec((1, TILE, TILE), lambda t, s: (jnp.maximum(t - 1, 0), 0, 0)),
            whole(wf),
            whole(wb),
            whole(spread),
            whole(place),
            whole(vec),
        ],
        out_specs=[
            pl.BlockSpec((2 * blocks, 32, 128), lambda t, s: (0, 0, 0)),
            pl.BlockSpec((3, C, 128), lambda t, s: (0, 0, 0)),
        ],
        scratch_shapes=[
            pltpu.VMEM((SPAN, 128), F32),
            pltpu.VMEM((2, SPAN, 128), F32),
            pltpu.VMEM((PLANE, 128), F32),
            pltpu.VMEM((2, PLANE, 128), F32),
            pltpu.VMEM((2, 3, PLANE, 128), F32),
            pltpu.VMEM((ROWS, 256), jnp.int32),
            pltpu.VMEM((ROWS, 256), BF),
            pltpu.VMEM((2, SLABS, ROWS, 128), BF),
            pltpu.VMEM((SPAN, 8, 128), F32),
            pltpu.VMEM((SPAN, 8, 128), F32),
            pltpu.VMEM((PLANE, 128), F32),
            pltpu.VMEM((PLANE, 128), F32),
            pltpu.VMEM((256, 768), F32),
            pltpu.VMEM((tiles * TILE + 2 * STEP, 128), F32),
            pltpu.VMEM((tiles * TILE + 2 * STEP, 128), F32),
        ],
    )
    return pl.pallas_call(
        functools.partial(tile_kernel, blocks, tiles),
        grid_spec=grid_spec,
        out_shape=[
            jax.ShapeDtypeStruct((2 * blocks, 32, 128), F32),
            jax.ShapeDtypeStruct((3, C, 128), F32),
        ],
        compiler_params=pltpu.CompilerParams(
            dimension_semantics=("arbitrary",), vmem_limit_bytes=48 * 1024 * 1024
        ),
    )(
        scalars,
        code_chunks,
        code_chunks,
        code_chunks,
        code_chunks,
        code_chunks,
        code_chunks,
        targets,
        wf,
        wb,
        spread,
        place,
        vec,
    )


def per_device(
    bins_x,
    proj_weight,
    convolution_weight,
    convolution_bias,
    readout,
    targets,
    block_order,
    band_reach,
):
    tiles = targets.shape[0]
    blocks = block_order.shape[0]
    axes = ("row", "diag")
    code_local = dot(bins_x, proj_weight).astype(BF)
    packed = jnp.concatenate([code_local[:32], code_local[32:]], axis=1)
    code_chunks = lax.all_to_all(
        jnp.broadcast_to(packed[None], (2 * blocks, 32, 128)), axes, 0, 0, tiled=True
    )
    positions = jnp.arange(blocks, dtype=jnp.int32)
    inverse = jnp.sum(
        jnp.where(block_order[:, None] == positions[None, :], positions[:, None], 0), axis=0
    )
    scalars = jnp.concatenate(
        [
            inverse,
            band_reach,
            jnp.stack([lax.axis_index("row"), lax.axis_index("diag")]).astype(jnp.int32),
        ]
    )
    taps = convolution_weight.reshape(3, 3, C, C).transpose(0, 1, 3, 2)
    wf = jnp.stack(
        [
            jnp.pad(taps, ((ii, 3 - ii), (jj, 1 - jj), (0, 0), (0, 0)))
            for ii in range(4)
            for jj in range(2)
        ],
        axis=3,
    ).reshape(768, 256)
    wb = wf.T
    vec = jnp.stack([jnp.tile(convolution_bias, 8), jnp.tile(readout, 8)])
    grads, tap_sums = run_tiles(scalars, code_chunks, targets, wf, wb, vec, blocks, tiles)
    tap_flat = (
        tap_sums[:, :, : 3 * C].reshape(3, C, 3, C).transpose(0, 2, 1, 3).reshape(2 * blocks, -1)
        / blocks
    )
    owned = tap_flat.shape[1]
    tap_rows = jnp.pad(tap_flat, ((0, 0), (0, 1024 - owned))).reshape(2 * blocks, 8, 128)
    terms = jnp.concatenate([grads.astype(BF), tap_rows.astype(BF)], axis=1)
    received = lax.all_to_all(terms, axes, 0, 0, tiled=True)
    mine = jnp.sum(received.astype(F32), axis=0)
    codes_grad = jnp.concatenate([mine[:32, :64], mine[:32, 64:]], axis=0)
    conv_grad = mine[32, :owned]
    return (codes_grad, conv_grad)


def solution(mesh):
    in_specs = (P(("row", "diag"), None), P(), P(), P(), P(), P("row", None, "diag"), P(), P())
    out_specs = (P(("row", "diag"), None), P(("row", "diag")))
    return jax.shard_map(
        per_device, mesh=mesh, in_specs=in_specs, out_specs=out_specs, check_vma=False
    )
```

```python
import functools

import jax
import jax.numpy as jnp
from jax import lax
from jax.experimental import pallas as pl
from jax.experimental.pallas import tpu as pltpu
from jax.sharding import PartitionSpec as P

C = 32
TILE = 128
STEP = 16
BAND = 16
PAIRS = TILE // (2 * STEP)
SLABS = TILE // STEP + 2
SPAN = TILE + 2 * STEP
PLANE = PAIRS * STEP
ROWS = STEP * PLANE
CHUNK = 512
MPIECE = 512
GROUP = 8

SQRT_HALF = 0.7071067811865476
HALF_LOG2E = -0.7213475204444817
INV_SQRT_TAU = 0.3989422804014327
BF = jnp.bfloat16
F32 = jnp.float32


def dot(a, b, dims=(((1,), (0,)), ((), ()))):
    return lax.dot_general(a, b, dims, preferred_element_type=F32)


def rows_of_sums(parts):
    x = [parts[n] for n in (3, 7, 1, 5, 2, 6, 0, 4)]
    s = lax.broadcasted_iota(jnp.int32, (8, 128), 0)
    upper, second, odd = s < 4, s // 2 % 2 == 1, s % 2 == 1
    x = [
        jnp.where(upper, p, q) + pltpu.roll(jnp.where(upper, q, p), 4, 0)
        for p, q in zip(x[0::2], x[1::2])
    ]
    x = [
        jnp.where(second, p + pltpu.roll(p, 2, 0), q + pltpu.roll(q, 6, 0))
        for p, q in zip(x[0::2], x[1::2])
    ]
    p, q = x
    return jnp.where(odd, p + pltpu.roll(p, 1, 0), q + pltpu.roll(q, 7, 0))


def lane_fold(x):
    x = x + pltpu.roll(x, 64, 1)
    return x + pltpu.roll(x, 32, 1)


def weave(*streams):
    streams = [list(x) for x in streams if x]
    order = sorted(
        ((n + 0.5) / len(x), m, n) for m, x in enumerate(streams) for n in range(len(x))
    )
    for _, m, n in order:
        streams[m][n]()


def tile_kernel(
    blocks,
    tiles,
    s_ref,
    row_prev,
    row_here,
    row_next,
    col_prev,
    col_here,
    col_next,
    tgt_ref,
    wf_ref,
    wb_ref,
    spread_ref,
    place_ref,
    pick_ref,
    vec_ref,
    grads_ref,
    taps_ref,
    u_row,
    w_row,
    uq_s,
    wq_s,
    wq_plain,
    mask_s,
    dist_s,
    tgt_s,
    x_s,
    c0_s,
    c1_s,
    acc_s,
    row_acc,
    col_acc,
):
    g = pl.program_id(0)
    new = g % 2
    old = 1 - new
    d = s_ref[2 * blocks + 1]
    first = s_ref[2 * blocks] * tiles

    @pl.when(g == 0)
    def _():
        acc_s[...] = jnp.zeros_like(acc_s)
        row_acc[...] = jnp.zeros_like(row_acc)
        col_acc[...] = jnp.zeros_like(col_acc)
        line = lax.broadcasted_iota(jnp.int32, (ROWS, 256), 0)
        lane = lax.broadcasted_iota(jnp.int32, (ROWS, 256), 1)
        r = line // PLANE
        jp = (line % PLANE) // STEP
        s = line % STEP
        ii = lane // 64
        jj = (lane // 32) % 2
        for ig in range(2):
            dist = TILE * d - 64 * ig + 32 * jp + s - r + 16 * (jj - ii)
            dist_s[ig] = jnp.where(dist >= 0, dist, 1 << 20).astype(F32)

    def codes(prev, here, after):
        left, right = spread_ref[0], spread_ref[1]
        return jnp.concatenate(
            [
                dot(prev[0], right),
                dot(here[0], left),
                dot(here[0], right),
                dot(here[1], left),
                dot(here[1], right),
                dot(after[0], left),
            ],
            axis=0,
        )

    def kind(i):
        return 0 if i == 0 else (2 if i == SLABS - 1 else 1)

    def prepare():
        row_codes = codes(row_prev, row_here, row_next)
        u_row[...] = row_codes[:, :128]
        w_row[new] = row_codes[:, 128:]
        col_codes = codes(col_prev, col_here, col_next).reshape(SLABS, STEP, 256)
        group = lax.broadcasted_iota(jnp.int32, (STEP, 256), 1) // C % 4
        for jp in range(PAIRS):
            window = col_codes[2 * jp]
            for m in range(1, 4):
                window = jnp.where(group == m, col_codes[2 * jp + m], window)
            uq_s[jp * STEP : (jp + 1) * STEP, :] = window[:, :128]
            wq_s[new, 1, jp * STEP : (jp + 1) * STEP, :] = window[:, 128:]
        line = lax.broadcasted_iota(jnp.int32, (PLANE, 128), 0)
        lane = lax.broadcasted_iota(jnp.int32, (PLANE, 128), 1)
        at_left = (line < STEP) & (lane < C)
        at_right = (line >= PLANE - STEP) & (lane >= 3 * C)
        for k in range(3):
            ar = first + g - 1 + k

            def inside(cb):
                ok = (ar >= 0) & (ar < blocks) & (cb >= ar) & (cb - ar < BAND) & (cb < blocks)
                return jnp.where(ok, 1.0, 0.0).astype(F32)

            bg = first + g + d
            mask_s[new, k] = jnp.where(
                at_left, inside(bg - 1), jnp.where(at_right, inside(bg + 1), inside(bg))
            )
        plain_w = wq_s[new, 1]
        wq_plain[...] = plain_w
        for k in range(3):
            wq_s[new, k] = plain_w * mask_s[new, k]

    def edged(value, which, k):
        mask = mask_s.at[which, k]
        if k != 1:
            return value * mask[...]
        return jnp.concatenate(
            [
                value[:STEP] * mask[:STEP, :],
                value[STEP : PLANE - STEP],
                value[PLANE - STEP :] * mask[PLANE - STEP :, :],
            ],
            axis=0,
        )

    def make_map(i, r):
        u = u_row[pl.ds(i * STEP + r, 1), :]
        w = w_row[new, pl.ds(i * STEP + r, 1), :]
        value = edged((u + uq_s[...]) + w * wq_plain[...], new, kind(i))
        x_s[new, i, pl.ds(r * PLANE, PLANE), :] = value.astype(BF)

    def make_maps(r, carry):
        for i in range(SLABS):
            make_map(i, r)
        return carry

    @pl.when(g == 0)
    def _():
        prepare()
        lax.fori_loop(0, STEP, make_maps, 0)

    bias = vec_ref[0:1, :]
    read = vec_ref[1:2, :]
    half_read = 0.5 * read
    read_density = read * INV_SQRT_TAU
    planes = CHUNK // PLANE

    def tile(t):
        prepare()
        a = first + t
        b = a + d
        reach = s_ref[blocks + a]
        c0_s[...] = jnp.zeros_like(c0_s)
        c1_s[...] = jnp.zeros_like(c1_s)

        turned = tgt_ref[0].astype(F32).T.reshape(PAIRS, 2, STEP, TILE)
        sides = [turned[:, jj].reshape(PLANE, TILE) for jj in range(2)]

        def make_target(r):
            for jj in range(2):
                value = sides[jj] if r == 0 else pltpu.roll(sides[jj], TILE - r, 1)
                tgt_s[r * PLANE : (r + 1) * PLANE, TILE * jj : TILE * (jj + 1)] = value.astype(BF)

        n = ROWS // CHUNK
        todo = [(ch, ig) for ch in range(n) for ig in range(2)]
        products, parts, grads, flips, sums = {}, {}, {}, {}, {}

        def pair(ch, k):
            rows = pl.ds(ch * CHUNK, CHUNK)
            return jnp.concatenate([x_s[old, 2 * k + i, rows, :] for i in range(2)], axis=1)

        def forward(m):
            ch, ig = todo[m]

            def first_pair():
                products[ch, 0] = dot(pair(ch, 0), wf_ref[:, 128:])

            def piece(k):
                products[ch, k] = dot(pair(ch, k), wf_ref[...])

            def last_pair():
                products[ch, 4] = dot(pair(ch, 4), wf_ref[:, :128])

            if ig == 0:
                return [first_pair] + [functools.partial(piece, k) for k in (1, 2)]
            return [functools.partial(piece, 3), last_pair]

        def summed(m, begin):
            ch, ig = todo[m]
            rows = slice(begin, begin + PLANE)
            if ig == 0:
                left, right = products[ch, 0][rows], products[ch, 2][rows, :128]
            else:
                left, right = products[ch, 2][rows, 128:], products[ch, 4][rows]
            middle = products[ch, 2 * ig + 1][rows]
            return jnp.concatenate([middle[:, :128] + left, middle[:, 128:] + right], axis=1)

        def slope(m):
            def piece(begin):
                v = summed(m, begin) + bias
                x = v * SQRT_HALF
                read_cdf = half_read * lax.erf(x) + half_read
                value = v * read_cdf
                high = value.astype(BF)
                low = (value - high.astype(F32)).astype(BF)
                parts[m, begin] = (
                    high,
                    low,
                    read_cdf + (read_density * v) * jnp.exp2(v * (v * HALF_LOG2E)),
                )

            return [functools.partial(piece, x) for x in range(0, CHUNK, PLANE)]

        def error(m):
            ch, ig = todo[m]
            farthest = jnp.where(b < blocks, reach, -1).astype(F32)
            out = {}

            def predict(base):
                pieces = [parts[m, base + x] for x in range(0, MPIECE, PLANE)]
                terms = jnp.concatenate(
                    [
                        jnp.concatenate([x[0] for x in pieces], axis=0),
                        jnp.concatenate([x[1] for x in pieces], axis=0),
                        tgt_s[pl.ds(ch * CHUNK + base, MPIECE), :],
                    ],
                    axis=1,
                )
                out[base] = dot(terms, place_ref[ig])

            def piece(begin):
                base = begin // MPIECE * MPIECE
                keep = dist_s[ig, pl.ds(ch * CHUNK + begin, PLANE), :] <= farthest
                miss = out[base][begin - base : begin - base + PLANE]
                err = jnp.where(keep, miss, 0.0) * TILE ** (-0.5)
                grads[m, begin] = (err * parts[m, begin][2]).astype(BF)

            todo_list = []
            for base in range(0, CHUNK, MPIECE):
                todo_list.append(functools.partial(predict, base))
                if base:
                    todo_list += [
                        functools.partial(piece, x) for x in range(base - MPIECE, base, PLANE)
                    ]
            todo_list += [
                functools.partial(piece, x) for x in range(CHUNK - MPIECE, CHUNK, PLANE)
            ]
            return todo_list

        def joined(m):
            whole = jnp.concatenate([grads[m, x] for x in range(0, CHUNK, PLANE)], axis=0)
            flips[m] = (whole, whole.T)

        def plain(m):
            ch, ig = todo[m]
            part = dot(pick_ref[:, pl.ds(ch * CHUNK, CHUNK)], flips[m][0])
            sums[ig] = part if ch == 0 else sums[ig] + part

        def plain_back():
            zero = jnp.zeros((2 * PLANE, 128), F32)
            four = [sums[0][:, :128], sums[0][:, 128:], sums[1][:, :128], sums[1][:, 128:]]
            four = [zero] + four + [zero]
            middle = None
            for k in range(SLABS // 2):
                both = jnp.concatenate([four[k], four[k + 1]], axis=1)
                high = both.astype(BF)
                low = (both - high.astype(F32)).astype(BF)
                out = dot(high, wb_ref[...]) + dot(low, wb_ref[...])
                for half in range(2):
                    i = 2 * k + half
                    value = out[:, 128 * half : 128 * (half + 1)]
                    rows = value[:PLANE].reshape(PAIRS, STEP, 128)
                    mask = mask_s.at[old, kind(i)]
                    total = rows[0] * mask[0:1, :] + rows[PAIRS - 1] * mask[PLANE - 1 : PLANE, :]
                    for jp in range(1, PAIRS - 1):
                        total = total + rows[jp] * mask[STEP : STEP + 1, :]
                    here = pl.ds(pl.multiple_of(t * TILE, TILE) + i * STEP, STEP)
                    row_acc[0, here, :] += total
                    if kind(i) == 1:
                        middle = value[PLANE:] if middle is None else middle + value[PLANE:]
                    else:
                        c0_s[...] += value[PLANE:] * mask[...]
            c0_s[...] += middle * mask_s[old, 1]

        def sides_of(m, which):
            ch, ig = todo[m]
            axis = 1 - which
            take = lambda n, h: lax.slice_in_dim(flips[n][which], 128 * h, 128 * h + 128, axis=axis)
            if ig == 0:
                return [(0, take(m, 0), slice(128, 256)), (1, flips[m][which], slice(0, 256))]
            return [
                (2, jnp.concatenate([take(m - 1, 1), take(m, 0)], axis=axis), slice(0, 256)),
                (3, flips[m][which], slice(0, 256)),
                (4, take(m, 1), slice(0, 128)),
            ]

        def taps(m):
            ch, ig = todo[m]

            def piece(n):
                k, lhs, where = sides_of(m, 1)[n]
                acc_s[where, :] += dot(lhs, pair(ch, k))

            return [functools.partial(piece, n) for n in range(2 + ig)]

        def back(m):
            ch, ig = todo[m]
            totals = {}

            def product(n):
                k, lhs, where = sides_of(m, 0)[n]
                totals[k] = dot(lhs, wb_ref[where, :])

            def piece(k, half, begin):
                i = 2 * k + half
                c1 = c1_s[kind(i)]
                wq = wq_s[old, kind(i)]
                r1 = []
                for rr in range(begin, begin + GROUP):
                    p = i * STEP + ch * planes + rr
                    dx = totals[k][rr * PLANE : (rr + 1) * PLANE, 128 * half : 128 * (half + 1)]
                    c1 = c1 + dx * w_row[old, p : p + 1, :]
                    r1.append(jnp.sum((dx * wq).reshape(PLANE // 8, 8, 128), axis=0))
                c1_s[kind(i)] = c1
                rows = pl.ds(pl.multiple_of(t * TILE, TILE) + i * STEP + ch * planes + begin, 8)
                row_acc[1, rows, :] += rows_of_sums(r1)

            out = []
            for n in range(2 + ig):
                out.append(functools.partial(product, n))
            for n in range(2 + ig):
                k = n + 2 * ig
                out += [
                    functools.partial(piece, k, half, x)
                    for half in range(2)
                    for x in range(0, planes, GROUP)
                ]
            return out

        targets = [functools.partial(make_target, r) for r in range(STEP)]
        fresh = [functools.partial(make_map, i, r) for r in range(STEP) for i in range(SLABS)]
        units = len(todo)
        steps = units + 3
        for m in range(steps):
            share = fresh[len(fresh) * m // steps : len(fresh) * (m + 1) // steps]
            tgt_now = targets[STEP * m // 2 : STEP * (m + 1) // 2] if m < 2 else []
            weave(
                forward(m) if m < units else [],
                slope(m - 1) if 0 <= m - 1 < units else [],
                error(m - 2) if 0 <= m - 2 < units else [],
                [functools.partial(joined, m - 3), functools.partial(plain, m - 3)]
                + taps(m - 3)
                + back(m - 3)
                if m >= 3
                else [],
                share,
                tgt_now,
            )

        here = pl.ds(pl.multiple_of(t * TILE, TILE), SPAN)
        group = lax.broadcasted_iota(jnp.int32, (STEP, 128), 1) // C

        def unwind(ref):
            pieces = []
            for m in range(PAIRS + 1):
                for odd in range(2):
                    value = jnp.zeros((STEP, 128), F32)
                    if m < PAIRS:
                        value = jnp.where(group == odd, ref[m * STEP : (m + 1) * STEP, :], value)
                    if m > 0:
                        value = jnp.where(
                            group == 2 + odd, ref[(m - 1) * STEP : m * STEP, :], value
                        )
                    pieces.append(value)
            return jnp.concatenate(pieces, axis=0)

        plain_back()
        c1_s[0] = (
            c1_s[0] * mask_s[old, 0] + c1_s[1] * mask_s[old, 1] + c1_s[2] * mask_s[old, 2]
        )
        col_acc[0, here, :] += unwind(c0_s)
        col_acc[1, here, :] += unwind(c1_s.at[0])

    @pl.when(g > 0)
    def _():
        tile(g - 1)

    @pl.when(g == tiles)
    def _():
        grads_ref[...] = jnp.zeros_like(grads_ref)
        low_half = lax.broadcasted_iota(jnp.int32, (32, 128), 1) < 64
        even = lax.broadcasted_iota(jnp.int32, row_acc.shape[1:], 1) // C % 2 == 0
        for acc_ref in (row_acc, col_acc):
            acc_ref[0] = jnp.where(even, lane_fold(acc_ref[0]), lane_fold(acc_ref[1]))


        def put(acc_ref, base, k, begin, count):
            n = base + k

            @pl.when((n >= 0) & (n < blocks))
            def _():
                slot = s_ref[n]
                for h in range(2):
                    top = acc_ref[0, pl.ds(begin + 64 * h, 32), :]
                    bottom = acc_ref[0, pl.ds(begin + 64 * h + 32, 32), :]
                    grads_ref[2 * slot + h] += jnp.where(low_half, top, bottom)

        for acc_ref, base in ((row_acc, first), (col_acc, first + d)):
            for k in range(tiles):
                put(acc_ref, base, k, STEP + k * TILE, TILE)

            @pl.when((base > 0) & (base <= blocks))
            def _():
                slot = s_ref[jnp.clip(base - 1, 0, blocks - 1)]
                grads_ref[2 * slot + 1, pl.ds(16, 16), :] += jnp.where(
                    low_half[:16], 0.0, acc_ref[0, 0:STEP, :]
                )

            @pl.when(base + tiles < blocks)
            def _():
                slot = s_ref[jnp.minimum(base + tiles, blocks - 1)]
                grads_ref[2 * slot, pl.ds(0, 16), :] += jnp.where(
                    low_half[:16], acc_ref[0, STEP + tiles * TILE : 2 * STEP + tiles * TILE, :], 0.0
                )

        for ty in range(3):
            total = (
                acc_s[64 * (2 - ty) : 64 * (3 - ty), :128]
                + acc_s[64 * (3 - ty) : 64 * (4 - ty), 128:]
            )
            taps_ref[ty] = total[:C] + pltpu.roll(total[C:], 96, 1)


def run_tiles(scalars, code_chunks, targets, wf, wb, vec, blocks, tiles):
    lane = jnp.arange(256, dtype=jnp.int32)
    source = lane // 128 * C + lane % C
    depth = jnp.arange(128, dtype=jnp.int32)
    spread = jnp.stack(
        [depth[:, None] == source[None, :], depth[:, None] == 64 + source[None, :]]
    ).astype(BF)
    ones = lane[:, None] // C == lane[None, :] // C
    place = jnp.stack(
        [
            jnp.concatenate(
                [ones.astype(BF), ones.astype(BF)]
                + [
                    -(
                        (depth[:, None] == 16 * (4 * ig + lane[None, :] // 64))
                        & (lane[None, :] // C % 2 == jj)
                    ).astype(BF)
                    for jj in range(2)
                ],
                axis=0,
            )
            for ig in range(2)
        ]
    )

    kept = jnp.arange(2 * PLANE, dtype=jnp.int32)[:, None]
    r, jp, s = (x[None, :] for x in (
        jnp.arange(ROWS, dtype=jnp.int32) // PLANE,
        jnp.arange(ROWS, dtype=jnp.int32) % PLANE // STEP,
        jnp.arange(ROWS, dtype=jnp.int32) % STEP,
    ))
    pick = ((kept == jp * STEP + r) | (kept == PLANE + jp * STEP + s)).astype(BF)

    def chunk_spec(offset, column, edge):
        def index(t, s):
            n = s[2 * blocks] * tiles + t + offset
            if column:
                n = n + s[2 * blocks + 1]
            n = s[jnp.clip(n, 0, blocks - 1)]
            if edge < 0:
                return (2 * n + 1, 1, 0)
            if edge > 0:
                return (2 * n, 0, 0)
            return (n, 0, 0)

        return pl.BlockSpec((1, STEP, 128) if edge else (2, 32, 128), index)

    def whole(x):
        zeros = (0,) * x.ndim
        return pl.BlockSpec(x.shape, lambda t, s: zeros)

    grid_spec = pltpu.PrefetchScalarGridSpec(
        num_scalar_prefetch=1,
        grid=(tiles + 1,),
        in_specs=[
            chunk_spec(-1, False, -1),
            chunk_spec(0, False, 0),
            chunk_spec(1, False, 1),
            chunk_spec(-1, True, -1),
            chunk_spec(0, True, 0),
            chunk_spec(1, True, 1),
            pl.BlockSpec((1, TILE, TILE), lambda t, s: (jnp.maximum(t - 1, 0), 0, 0)),
            whole(wf),
            whole(wb),
            whole(spread),
            whole(place),
            whole(pick),
            whole(vec),
        ],
        out_specs=[
            pl.BlockSpec((2 * blocks, 32, 128), lambda t, s: (0, 0, 0)),
            pl.BlockSpec((3, C, 128), lambda t, s: (0, 0, 0)),
        ],
        scratch_shapes=[
            pltpu.VMEM((SPAN, 128), F32),
            pltpu.VMEM((2, SPAN, 128), F32),
            pltpu.VMEM((PLANE, 128), F32),
            pltpu.VMEM((2, 3, PLANE, 128), F32),
            pltpu.VMEM((PLANE, 128), F32),
            pltpu.VMEM((2, 3, PLANE, 128), F32),
            pltpu.VMEM((2, ROWS, 256), F32),
            pltpu.VMEM((ROWS, 256), BF),
            pltpu.VMEM((2, SLABS, ROWS, 128), BF),
            pltpu.VMEM((PLANE, 128), F32),
            pltpu.VMEM((3, PLANE, 128), F32),
            pltpu.VMEM((256, 256), F32),
            pltpu.VMEM((2, tiles * TILE + 2 * STEP, 128), F32),
            pltpu.VMEM((2, tiles * TILE + 2 * STEP, 128), F32),
        ],
    )
    return pl.pallas_call(
        functools.partial(tile_kernel, blocks, tiles),
        grid_spec=grid_spec,
        out_shape=[
            jax.ShapeDtypeStruct((2 * blocks, 32, 128), F32),
            jax.ShapeDtypeStruct((3, C, 128), F32),
        ],
        compiler_params=pltpu.CompilerParams(
            dimension_semantics=("arbitrary",), vmem_limit_bytes=48 * 1024 * 1024
        ),
    )(
        scalars,
        code_chunks,
        code_chunks,
        code_chunks,
        code_chunks,
        code_chunks,
        code_chunks,
        targets,
        wf,
        wb,
        spread,
        place,
        pick,
        vec,
    )


def per_device(
    bins_x,
    proj_weight,
    convolution_weight,
    convolution_bias,
    readout,
    targets,
    block_order,
    band_reach,
):
    tiles = targets.shape[0]
    blocks = block_order.shape[0]
    axes = ("row", "diag")
    code_local = dot(bins_x, proj_weight).astype(BF)
    packed = jnp.concatenate([code_local[:32], code_local[32:]], axis=1)
    code_chunks = lax.all_to_all(
        jnp.broadcast_to(packed[None], (2 * blocks, 32, 128)), axes, 0, 0, tiled=True
    )
    positions = jnp.arange(blocks, dtype=jnp.int32)
    inverse = jnp.sum(
        jnp.where(block_order[:, None] == positions[None, :], positions[:, None], 0), axis=0
    )
    scalars = jnp.concatenate(
        [
            inverse,
            band_reach,
            jnp.stack([lax.axis_index("row"), lax.axis_index("diag")]).astype(jnp.int32),
        ]
    )
    taps = convolution_weight.reshape(3, 3, C, C).transpose(0, 1, 3, 2)
    wf = jnp.stack(
        [
            jnp.pad(
                taps[max(0, 2 - rho) : 4 - rho],
                ((max(0, rho - 2), max(0, 1 - rho)), (jj, 1 - jj), (0, 0), (0, 0)),
            )
            for rho in range(4)
            for jj in range(2)
        ],
        axis=3,
    ).reshape(256, 256)
    wb = wf.T
    vec = jnp.stack([jnp.tile(convolution_bias, 8), jnp.tile(readout, 8)])
    grads, tap_sums = run_tiles(scalars, code_chunks, targets, wf, wb, vec, blocks, tiles)
    tap_flat = (
        tap_sums[:, :, : 3 * C].reshape(3, C, 3, C).transpose(0, 2, 1, 3).reshape(2 * blocks, -1)
        / blocks
    )
    owned = tap_flat.shape[1]
    tap_rows = jnp.pad(tap_flat, ((0, 0), (0, 1024 - owned))).reshape(2 * blocks, 8, 128)
    terms = jnp.concatenate([grads.astype(BF), tap_rows.astype(BF)], axis=1)
    received = lax.all_to_all(terms, axes, 0, 0, tiled=True)
    mine = jnp.sum(received.astype(F32), axis=0)
    codes_grad = jnp.concatenate([mine[:32, :64], mine[:32, 64:]], axis=0)
    conv_grad = mine[32, :owned]
    return (codes_grad, conv_grad)


def solution(mesh):
    in_specs = (P(("row", "diag"), None), P(), P(), P(), P(), P("row", None, "diag"), P(), P())
    out_specs = (P(("row", "diag"), None), P(("row", "diag")))
    return jax.shard_map(
        per_device, mesh=mesh, in_specs=in_specs, out_specs=out_specs, check_vma=False
    )
```

```python
import functools

import jax
import jax.numpy as jnp
from jax import lax
from jax.experimental import pallas as pl
from jax.experimental.pallas import tpu as pltpu
from jax.sharding import PartitionSpec as P

C = 32
TILE = 128
STEP = 16
BAND = 16
PAIRS = TILE // (2 * STEP)
SLABS = TILE // STEP + 2
SPAN = TILE + 2 * STEP
PLANE = PAIRS * STEP
ROWS = STEP * PLANE
CHUNK = 512
MPIECE = 512
GROUP = 8

SQRT_HALF = 0.7071067811865476
HALF_LOG2E = -0.7213475204444817
INV_SQRT_TAU = 0.3989422804014327
BF = jnp.bfloat16
F32 = jnp.float32


def dot(a, b, dims=(((1,), (0,)), ((), ()))):
    return lax.dot_general(a, b, dims, preferred_element_type=F32)


def rows_of_sums(parts):
    x = [parts[n] for n in (3, 7, 1, 5, 2, 6, 0, 4)]
    s = lax.broadcasted_iota(jnp.int32, (8, 128), 0)
    upper, second, odd = s < 4, s // 2 % 2 == 1, s % 2 == 1
    x = [
        jnp.where(upper, p, q) + pltpu.roll(jnp.where(upper, q, p), 4, 0)
        for p, q in zip(x[0::2], x[1::2])
    ]
    x = [
        jnp.where(second, p + pltpu.roll(p, 2, 0), q + pltpu.roll(q, 6, 0))
        for p, q in zip(x[0::2], x[1::2])
    ]
    p, q = x
    return jnp.where(odd, p + pltpu.roll(p, 1, 0), q + pltpu.roll(q, 7, 0))


def lane_fold(x):
    x = x + pltpu.roll(x, 64, 1)
    return x + pltpu.roll(x, 32, 1)


def weave(*streams):
    streams = [list(x) for x in streams if x]
    order = sorted(
        ((n + 0.5) / len(x), m, n) for m, x in enumerate(streams) for n in range(len(x))
    )
    for _, m, n in order:
        streams[m][n]()


def tile_kernel(
    blocks,
    tiles,
    s_ref,
    mine_ref,
    theirs_ref,
    tgt_ref,
    wf_ref,
    wb_ref,
    spread_ref,
    place_ref,
    pick_ref,
    vec_ref,
    keep_ref,
    send_ref,
    taps_ref,
    u_row,
    w_row,
    uq_s,
    wq_s,
    wq_plain,
    mask_s,
    dist_s,
    tgt_s,
    x_s,
    c0_s,
    c1_s,
    acc_s,
    row_acc,
    col_acc,
    grads_s,
):
    g = pl.program_id(0)
    new = g % 2
    old = 1 - new
    d = s_ref[2 * blocks + 1]
    first = s_ref[2 * blocks] * tiles

    @pl.when(g == 0)
    def _():
        acc_s[...] = jnp.zeros_like(acc_s)
        row_acc[...] = jnp.zeros_like(row_acc)
        col_acc[...] = jnp.zeros_like(col_acc)
        line = lax.broadcasted_iota(jnp.int32, (ROWS, 256), 0)
        lane = lax.broadcasted_iota(jnp.int32, (ROWS, 256), 1)
        r = line // PLANE
        jp = (line % PLANE) // STEP
        s = line % STEP
        ii = lane // 64
        jj = (lane // 32) % 2
        for ig in range(2):
            dist = TILE * d - 64 * ig + 32 * jp + s - r + 16 * (jj - ii)
            dist_s[ig] = jnp.where(dist >= 0, dist, 1 << 20).astype(F32)

    core = s_ref[2 * blocks + 1] % 2

    def codes(n):
        left, right = spread_ref[0], spread_ref[1]

        def chunk(block, h, rows):
            slot = s_ref[jnp.clip(block, 0, blocks - 1)]
            return jnp.where(core == h, mine_ref[slot, rows, :], theirs_ref[slot, rows, :])

        first_half, second_half = (chunk(n, h, slice(0, 32)) for h in range(2))
        return jnp.concatenate(
            [
                dot(chunk(n - 1, 1, slice(16, 32)), right),
                dot(first_half, left),
                dot(first_half, right),
                dot(second_half, left),
                dot(second_half, right),
                dot(chunk(n + 1, 0, slice(0, 16)), left),
            ],
            axis=0,
        )

    def kind(i):
        return 0 if i == 0 else (2 if i == SLABS - 1 else 1)

    def prepare():
        row_codes = codes(first + g)
        u_row[...] = row_codes[:, :128]
        w_row[new] = row_codes[:, 128:]
        col_codes = codes(first + g + d).reshape(SLABS, STEP, 256)
        group = lax.broadcasted_iota(jnp.int32, (STEP, 256), 1) // C % 4
        for jp in range(PAIRS):
            window = col_codes[2 * jp]
            for m in range(1, 4):
                window = jnp.where(group == m, col_codes[2 * jp + m], window)
            uq_s[jp * STEP : (jp + 1) * STEP, :] = window[:, :128]
            wq_s[new, 1, jp * STEP : (jp + 1) * STEP, :] = window[:, 128:]
        line = lax.broadcasted_iota(jnp.int32, (PLANE, 128), 0)
        lane = lax.broadcasted_iota(jnp.int32, (PLANE, 128), 1)
        at_left = (line < STEP) & (lane < C)
        at_right = (line >= PLANE - STEP) & (lane >= 3 * C)
        for k in range(3):
            ar = first + g - 1 + k

            def inside(cb):
                ok = (ar >= 0) & (ar < blocks) & (cb >= ar) & (cb - ar < BAND) & (cb < blocks)
                return jnp.where(ok, 1.0, 0.0).astype(F32)

            bg = first + g + d
            mask_s[new, k] = jnp.where(
                at_left, inside(bg - 1), jnp.where(at_right, inside(bg + 1), inside(bg))
            )
        plain_w = wq_s[new, 1]
        wq_plain[...] = plain_w
        for k in range(3):
            wq_s[new, k] = plain_w * mask_s[new, k]

    def edged(value, which, k):
        mask = mask_s.at[which, k]
        if k != 1:
            return value * mask[...]
        return jnp.concatenate(
            [
                value[:STEP] * mask[:STEP, :],
                value[STEP : PLANE - STEP],
                value[PLANE - STEP :] * mask[PLANE - STEP :, :],
            ],
            axis=0,
        )

    def make_map(i, r):
        u = u_row[pl.ds(i * STEP + r, 1), :]
        w = w_row[new, pl.ds(i * STEP + r, 1), :]
        value = edged((u + uq_s[...]) + w * wq_plain[...], new, kind(i))
        x_s[new, i, pl.ds(r * PLANE, PLANE), :] = value.astype(BF)

    def make_maps(r, carry):
        for i in range(SLABS):
            make_map(i, r)
        return carry

    @pl.when(g == 0)
    def _():
        prepare()
        lax.fori_loop(0, STEP, make_maps, 0)

    bias = vec_ref[0:1, :]
    read = vec_ref[1:2, :]
    half_read = 0.5 * read
    read_density = read * INV_SQRT_TAU
    planes = CHUNK // PLANE

    def tile(t):
        prepare()
        a = first + t
        b = a + d
        reach = s_ref[blocks + a]
        c0_s[...] = jnp.zeros_like(c0_s)
        c1_s[...] = jnp.zeros_like(c1_s)

        turned = tgt_ref[t].astype(F32).T.reshape(PAIRS, 2, STEP, TILE)
        sides = [turned[:, jj].reshape(PLANE, TILE) for jj in range(2)]

        def make_target(r):
            for jj in range(2):
                value = sides[jj] if r == 0 else pltpu.roll(sides[jj], TILE - r, 1)
                tgt_s[r * PLANE : (r + 1) * PLANE, TILE * jj : TILE * (jj + 1)] = value.astype(BF)

        n = ROWS // CHUNK
        todo = [(ch, ig) for ch in range(n) for ig in range(2)]
        products, parts, grads, flips, sums = {}, {}, {}, {}, {}

        def pair(ch, k):
            rows = pl.ds(ch * CHUNK, CHUNK)
            return jnp.concatenate([x_s[old, 2 * k + i, rows, :] for i in range(2)], axis=1)

        def forward(m):
            ch, ig = todo[m]

            def first_pair():
                products[ch, 0] = dot(pair(ch, 0), wf_ref[:, 128:])

            def piece(k):
                products[ch, k] = dot(pair(ch, k), wf_ref[...])

            def last_pair():
                products[ch, 4] = dot(pair(ch, 4), wf_ref[:, :128])

            if ig == 0:
                return [first_pair] + [functools.partial(piece, k) for k in (1, 2)]
            return [functools.partial(piece, 3), last_pair]

        def summed(m, begin):
            ch, ig = todo[m]
            rows = slice(begin, begin + PLANE)
            if ig == 0:
                left, right = products[ch, 0][rows], products[ch, 2][rows, :128]
            else:
                left, right = products[ch, 2][rows, 128:], products[ch, 4][rows]
            middle = products[ch, 2 * ig + 1][rows]
            return jnp.concatenate([middle[:, :128] + left, middle[:, 128:] + right], axis=1)

        def slope(m):
            def piece(begin):
                v = summed(m, begin) + bias
                x = v * SQRT_HALF
                read_cdf = half_read * lax.erf(x) + half_read
                value = v * read_cdf
                high = value.astype(BF)
                low = (value - high.astype(F32)).astype(BF)
                parts[m, begin] = (
                    high,
                    low,
                    read_cdf + (read_density * v) * jnp.exp2(v * (v * HALF_LOG2E)),
                )

            return [functools.partial(piece, x) for x in range(0, CHUNK, PLANE)]

        def error(m):
            ch, ig = todo[m]
            farthest = jnp.where(b < blocks, reach, -1).astype(F32)
            out = {}

            def predict(base):
                pieces = [parts[m, base + x] for x in range(0, MPIECE, PLANE)]
                terms = jnp.concatenate(
                    [
                        jnp.concatenate([x[0] for x in pieces], axis=0),
                        jnp.concatenate([x[1] for x in pieces], axis=0),
                        tgt_s[pl.ds(ch * CHUNK + base, MPIECE), :],
                    ],
                    axis=1,
                )
                out[base] = dot(terms, place_ref[ig])

            def piece(begin):
                base = begin // MPIECE * MPIECE
                keep = dist_s[ig, pl.ds(ch * CHUNK + begin, PLANE), :] <= farthest
                miss = out[base][begin - base : begin - base + PLANE]
                err = jnp.where(keep, miss, 0.0) * TILE ** (-0.5)
                grads[m, begin] = (err * parts[m, begin][2]).astype(BF)

            todo_list = []
            for base in range(0, CHUNK, MPIECE):
                todo_list.append(functools.partial(predict, base))
                if base:
                    todo_list += [
                        functools.partial(piece, x) for x in range(base - MPIECE, base, PLANE)
                    ]
            todo_list += [
                functools.partial(piece, x) for x in range(CHUNK - MPIECE, CHUNK, PLANE)
            ]
            return todo_list

        def joined(m):
            whole = jnp.concatenate([grads[m, x] for x in range(0, CHUNK, PLANE)], axis=0)
            flips[m] = (whole, whole.T)

        def plain(m):
            ch, ig = todo[m]
            part = dot(pick_ref[:, pl.ds(ch * CHUNK, CHUNK)], flips[m][0])
            sums[ig] = part if ch == 0 else sums[ig] + part

        def plain_back():
            zero = jnp.zeros((2 * PLANE, 128), F32)
            four = [sums[0][:, :128], sums[0][:, 128:], sums[1][:, :128], sums[1][:, 128:]]
            four = [zero] + four + [zero]
            middle = None
            for k in range(SLABS // 2):
                both = jnp.concatenate([four[k], four[k + 1]], axis=1)
                high = both.astype(BF)
                low = (both - high.astype(F32)).astype(BF)
                out = dot(high, wb_ref[...]) + dot(low, wb_ref[...])
                for half in range(2):
                    i = 2 * k + half
                    value = out[:, 128 * half : 128 * (half + 1)]
                    rows = value[:PLANE].reshape(PAIRS, STEP, 128)
                    mask = mask_s.at[old, kind(i)]
                    total = rows[0] * mask[0:1, :] + rows[PAIRS - 1] * mask[PLANE - 1 : PLANE, :]
                    for jp in range(1, PAIRS - 1):
                        total = total + rows[jp] * mask[STEP : STEP + 1, :]
                    here = pl.ds(pl.multiple_of(t * TILE, TILE) + i * STEP, STEP)
                    row_acc[0, here, :] += total
                    if kind(i) == 1:
                        middle = value[PLANE:] if middle is None else middle + value[PLANE:]
                    else:
                        c0_s[...] += value[PLANE:] * mask[...]
            c0_s[...] += middle * mask_s[old, 1]

        def sides_of(m, which):
            ch, ig = todo[m]
            axis = 1 - which
            take = lambda n, h: lax.slice_in_dim(flips[n][which], 128 * h, 128 * h + 128, axis=axis)
            if ig == 0:
                return [(0, take(m, 0), slice(128, 256)), (1, flips[m][which], slice(0, 256))]
            return [
                (2, jnp.concatenate([take(m - 1, 1), take(m, 0)], axis=axis), slice(0, 256)),
                (3, flips[m][which], slice(0, 256)),
                (4, take(m, 1), slice(0, 128)),
            ]

        def taps(m):
            ch, ig = todo[m]

            def piece(n):
                k, lhs, where = sides_of(m, 1)[n]
                acc_s[where, :] += dot(lhs, pair(ch, k))

            return [functools.partial(piece, n) for n in range(2 + ig)]

        def back(m):
            ch, ig = todo[m]
            totals = {}

            def product(n):
                k, lhs, where = sides_of(m, 0)[n]
                totals[k] = dot(lhs, wb_ref[where, :])

            def piece(k, half, begin):
                i = 2 * k + half
                c1 = c1_s[kind(i)]
                wq = wq_s[old, kind(i)]
                r1 = []
                for rr in range(begin, begin + GROUP):
                    p = i * STEP + ch * planes + rr
                    dx = totals[k][rr * PLANE : (rr + 1) * PLANE, 128 * half : 128 * (half + 1)]
                    c1 = c1 + dx * w_row[old, p : p + 1, :]
                    r1.append(jnp.sum((dx * wq).reshape(PLANE // 8, 8, 128), axis=0))
                c1_s[kind(i)] = c1
                rows = pl.ds(pl.multiple_of(t * TILE, TILE) + i * STEP + ch * planes + begin, 8)
                row_acc[1, rows, :] += rows_of_sums(r1)

            out = []
            for n in range(2 + ig):
                out.append(functools.partial(product, n))
            for n in range(2 + ig):
                k = n + 2 * ig
                out += [
                    functools.partial(piece, k, half, x)
                    for half in range(2)
                    for x in range(0, planes, GROUP)
                ]
            return out

        targets = [functools.partial(make_target, r) for r in range(STEP)]
        fresh = [functools.partial(make_map, i, r) for r in range(STEP) for i in range(SLABS)]
        units = len(todo)
        steps = units + 3
        for m in range(steps):
            share = fresh[len(fresh) * m // steps : len(fresh) * (m + 1) // steps]
            tgt_now = targets[STEP * m // 2 : STEP * (m + 1) // 2] if m < 2 else []
            weave(
                forward(m) if m < units else [],
                slope(m - 1) if 0 <= m - 1 < units else [],
                error(m - 2) if 0 <= m - 2 < units else [],
                [functools.partial(joined, m - 3), functools.partial(plain, m - 3)]
                + taps(m - 3)
                + back(m - 3)
                if m >= 3
                else [],
                share,
                tgt_now,
            )

        here = pl.ds(pl.multiple_of(t * TILE, TILE), SPAN)
        group = lax.broadcasted_iota(jnp.int32, (STEP, 128), 1) // C

        def unwind(ref):
            pieces = []
            for m in range(PAIRS + 1):
                for odd in range(2):
                    value = jnp.zeros((STEP, 128), F32)
                    if m < PAIRS:
                        value = jnp.where(group == odd, ref[m * STEP : (m + 1) * STEP, :], value)
                    if m > 0:
                        value = jnp.where(
                            group == 2 + odd, ref[(m - 1) * STEP : m * STEP, :], value
                        )
                    pieces.append(value)
            return jnp.concatenate(pieces, axis=0)

        plain_back()
        c1_s[0] = (
            c1_s[0] * mask_s[old, 0] + c1_s[1] * mask_s[old, 1] + c1_s[2] * mask_s[old, 2]
        )
        col_acc[0, here, :] += unwind(c0_s)
        col_acc[1, here, :] += unwind(c1_s.at[0])

    @pl.when(g > 0)
    def _():
        tile(g - 1)

    @pl.when(g == tiles)
    def _():
        grads_s[...] = jnp.zeros_like(grads_s)
        low_half = lax.broadcasted_iota(jnp.int32, (32, 128), 1) < 64
        even = lax.broadcasted_iota(jnp.int32, row_acc.shape[1:], 1) // C % 2 == 0
        for acc_ref in (row_acc, col_acc):
            acc_ref[0] = jnp.where(even, lane_fold(acc_ref[0]), lane_fold(acc_ref[1]))


        def put(acc_ref, base, k, begin, count):
            n = base + k

            @pl.when((n >= 0) & (n < blocks))
            def _():
                slot = s_ref[n]
                for h in range(2):
                    top = acc_ref[0, pl.ds(begin + 64 * h, 32), :]
                    bottom = acc_ref[0, pl.ds(begin + 64 * h + 32, 32), :]
                    grads_s[(h + core) % 2, slot] += jnp.where(low_half, top, bottom)

        for acc_ref, base in ((row_acc, first), (col_acc, first + d)):
            for k in range(tiles):
                put(acc_ref, base, k, STEP + k * TILE, TILE)

            @pl.when((base > 0) & (base <= blocks))
            def _():
                slot = s_ref[jnp.clip(base - 1, 0, blocks - 1)]
                grads_s[(1 + core) % 2, slot, pl.ds(16, 16), :] += jnp.where(
                    low_half[:16], 0.0, acc_ref[0, 0:STEP, :]
                )

            @pl.when(base + tiles < blocks)
            def _():
                slot = s_ref[jnp.minimum(base + tiles, blocks - 1)]
                grads_s[core, slot, pl.ds(0, 16), :] += jnp.where(
                    low_half[:16], acc_ref[0, STEP + tiles * TILE : 2 * STEP + tiles * TILE, :], 0.0
                )

        keep_ref[...] = grads_s[0]
        send_ref[...] = grads_s[1].astype(BF)
        for ty in range(3):
            total = (
                acc_s[64 * (2 - ty) : 64 * (3 - ty), :128]
                + acc_s[64 * (3 - ty) : 64 * (4 - ty), 128:]
            )
            taps_ref[ty] = total[:C] + pltpu.roll(total[C:], 96, 1)


def run_tiles(scalars, mine, theirs, targets, wf, wb, vec, blocks, tiles):
    lane = jnp.arange(256, dtype=jnp.int32)
    source = lane // 128 * C + lane % C
    depth = jnp.arange(128, dtype=jnp.int32)
    spread = jnp.stack(
        [depth[:, None] == source[None, :], depth[:, None] == 64 + source[None, :]]
    ).astype(BF)
    ones = lane[:, None] // C == lane[None, :] // C
    place = jnp.stack(
        [
            jnp.concatenate(
                [ones.astype(BF), ones.astype(BF)]
                + [
                    -(
                        (depth[:, None] == 16 * (4 * ig + lane[None, :] // 64))
                        & (lane[None, :] // C % 2 == jj)
                    ).astype(BF)
                    for jj in range(2)
                ],
                axis=0,
            )
            for ig in range(2)
        ]
    )

    kept = jnp.arange(2 * PLANE, dtype=jnp.int32)[:, None]
    r, jp, s = (x[None, :] for x in (
        jnp.arange(ROWS, dtype=jnp.int32) // PLANE,
        jnp.arange(ROWS, dtype=jnp.int32) % PLANE // STEP,
        jnp.arange(ROWS, dtype=jnp.int32) % STEP,
    ))
    pick = ((kept == jp * STEP + r) | (kept == PLANE + jp * STEP + s)).astype(BF)

    def whole(x):
        zeros = (0,) * x.ndim
        return pl.BlockSpec(x.shape, lambda t, s: zeros)

    grid_spec = pltpu.PrefetchScalarGridSpec(
        num_scalar_prefetch=1,
        grid=(tiles + 1,),
        in_specs=[
            whole(mine),
            whole(theirs),
            whole(targets),
            whole(wf),
            whole(wb),
            whole(spread),
            whole(place),
            whole(pick),
            whole(vec),
        ],
        out_specs=[
            pl.BlockSpec((blocks, 32, 128), lambda t, s: (0, 0, 0)),
            pl.BlockSpec((blocks, 32, 128), lambda t, s: (0, 0, 0)),
            pl.BlockSpec((3, C, 128), lambda t, s: (0, 0, 0)),
        ],
        scratch_shapes=[
            pltpu.VMEM((SPAN, 128), F32),
            pltpu.VMEM((2, SPAN, 128), F32),
            pltpu.VMEM((PLANE, 128), F32),
            pltpu.VMEM((2, 3, PLANE, 128), F32),
            pltpu.VMEM((PLANE, 128), F32),
            pltpu.VMEM((2, 3, PLANE, 128), F32),
            pltpu.VMEM((2, ROWS, 256), F32),
            pltpu.VMEM((ROWS, 256), BF),
            pltpu.VMEM((2, SLABS, ROWS, 128), BF),
            pltpu.VMEM((PLANE, 128), F32),
            pltpu.VMEM((3, PLANE, 128), F32),
            pltpu.VMEM((256, 256), F32),
            pltpu.VMEM((2, tiles * TILE + 2 * STEP, 128), F32),
            pltpu.VMEM((2, tiles * TILE + 2 * STEP, 128), F32),
            pltpu.VMEM((2, blocks, 32, 128), F32),
        ],
    )
    return pl.pallas_call(
        functools.partial(tile_kernel, blocks, tiles),
        grid_spec=grid_spec,
        out_shape=[
            jax.ShapeDtypeStruct((blocks, 32, 128), F32),
            jax.ShapeDtypeStruct((blocks, 32, 128), BF),
            jax.ShapeDtypeStruct((3, C, 128), F32),
        ],
        compiler_params=pltpu.CompilerParams(
            dimension_semantics=("arbitrary",), vmem_limit_bytes=48 * 1024 * 1024
        ),
    )(
        scalars,
        mine,
        theirs,
        targets,
        wf,
        wb,
        spread,
        place,
        pick,
        vec,
    )


def per_device(
    bins_x,
    proj_weight,
    convolution_weight,
    convolution_bias,
    readout,
    targets,
    block_order,
    band_reach,
):
    tiles = targets.shape[0]
    blocks = block_order.shape[0]
    axes = ("row", "diag")
    code_local = dot(bins_x, proj_weight).astype(BF)
    packed = jnp.concatenate([code_local[:32], code_local[32:]], axis=1)
    core = lax.axis_index("diag") % 2
    peers = lax.axis_size("row") * lax.axis_size("diag")
    same_core = [list(range(c, peers, 2)) for c in range(2)]
    swap = [(i, i ^ 1) for i in range(lax.axis_size("diag"))]
    mine = lax.all_to_all(
        jnp.broadcast_to(packed[None], (blocks, 32, 128)),
        axes,
        0,
        0,
        axis_index_groups=same_core,
        tiled=True,
    )
    theirs = lax.ppermute(mine, "diag", swap)
    positions = jnp.arange(blocks, dtype=jnp.int32)
    inverse = jnp.sum(
        jnp.where(block_order[:, None] == positions[None, :], positions[:, None], 0), axis=0
    )
    scalars = jnp.concatenate(
        [
            inverse,
            band_reach,
            jnp.stack([lax.axis_index("row"), lax.axis_index("diag")]).astype(jnp.int32),
        ]
    )
    taps = convolution_weight.reshape(3, 3, C, C).transpose(0, 1, 3, 2)
    wf = jnp.stack(
        [
            jnp.pad(
                taps[max(0, 2 - rho) : 4 - rho],
                ((max(0, rho - 2), max(0, 1 - rho)), (jj, 1 - jj), (0, 0), (0, 0)),
            )
            for rho in range(4)
            for jj in range(2)
        ],
        axis=3,
    ).reshape(256, 256)
    wb = wf.T
    vec = jnp.stack([jnp.tile(convolution_bias, 8), jnp.tile(readout, 8)])
    keep, send, tap_sums = run_tiles(scalars, mine, theirs, targets, wf, wb, vec, blocks, tiles)
    tap_flat = (
        tap_sums[:, :, : 3 * C].reshape(3, C, 3, C).transpose(0, 2, 1, 3).reshape(2 * blocks, -1)
        / blocks
    )
    owned = tap_flat.shape[1]
    tap_rows = jnp.pad(tap_flat, ((0, 0), (0, 1024 - owned))).reshape(blocks, 2, 8, 128)
    tap_first, tap_second = tap_rows[:, 0], tap_rows[:, 1]
    tap_keep = jnp.where(core == 0, tap_first, tap_second)
    tap_send = jnp.where(core == 0, tap_second, tap_first)
    sent = jnp.concatenate([send, tap_send.astype(BF)], axis=1)
    other = lax.ppermute(sent, "diag", swap)
    terms = jnp.concatenate([keep, tap_keep], axis=1) + other.astype(F32)
    received = lax.all_to_all(
        terms.astype(BF), axes, 0, 0, axis_index_groups=same_core, tiled=True
    )
    total = jnp.sum(received.astype(F32), axis=0)
    codes_grad = jnp.concatenate([total[:32, :64], total[:32, 64:]], axis=0)
    conv_grad = total[32, :owned]
    return (codes_grad, conv_grad)


def solution(mesh):
    in_specs = (P(("row", "diag"), None), P(), P(), P(), P(), P("row", None, "diag"), P(), P())
    out_specs = (P(("row", "diag"), None), P(("row", "diag")))
    return jax.shard_map(
        per_device, mesh=mesh, in_specs=in_specs, out_specs=out_specs, check_vma=False
    )
```

```python
import functools

import jax
import jax.numpy as jnp
from jax import lax
from jax.experimental import pallas as pl
from jax.experimental.pallas import tpu as pltpu
from jax.sharding import PartitionSpec as P

C = 32
TILE = 128
STEP = 16
BAND = 16
PAIRS = TILE // (2 * STEP)
SLABS = TILE // STEP + 2
SPAN = TILE + 2 * STEP
PLANE = PAIRS * STEP
ROWS = STEP * PLANE
CHUNK = 512
MPIECE = 512
GROUP = 8
TOGETHER = 1

SQRT_HALF = 0.7071067811865476
HALF_LOG2E = -0.7213475204444817
INV_SQRT_TAU = 0.3989422804014327
BF = jnp.bfloat16
F32 = jnp.float32


def dot(a, b, dims=(((1,), (0,)), ((), ()))):
    return lax.dot_general(a, b, dims, preferred_element_type=F32)


def rows_of_sums(parts):
    x = [parts[n] for n in (3, 7, 1, 5, 2, 6, 0, 4)]
    s = lax.broadcasted_iota(jnp.int32, (8, 128), 0)
    upper, second, odd = s < 4, s // 2 % 2 == 1, s % 2 == 1
    x = [
        jnp.where(upper, p, q) + pltpu.roll(jnp.where(upper, q, p), 4, 0)
        for p, q in zip(x[0::2], x[1::2])
    ]
    x = [
        jnp.where(second, p + pltpu.roll(p, 2, 0), q + pltpu.roll(q, 6, 0))
        for p, q in zip(x[0::2], x[1::2])
    ]
    p, q = x
    return jnp.where(odd, p + pltpu.roll(p, 1, 0), q + pltpu.roll(q, 7, 0))


def lane_fold(x):
    x = x + pltpu.roll(x, 64, 1)
    return x + pltpu.roll(x, 32, 1)


def weave(*streams):
    streams = [list(x) for x in streams if x]
    order = sorted(
        ((n + 0.5) / len(x), m, n) for m, x in enumerate(streams) for n in range(len(x))
    )
    for _, m, n in order:
        streams[m][n]()


def tile_kernel(
    blocks,
    tiles,
    s_ref,
    mine_ref,
    theirs_ref,
    tgt_ref,
    wf_ref,
    wb_ref,
    spread_ref,
    place_ref,
    pick_ref,
    vec_ref,
    keep_ref,
    send_ref,
    taps_ref,
    u_row,
    w_row,
    uq_s,
    wq_s,
    wq_plain,
    mask_s,
    dist_s,
    tgt_s,
    x_s,
    c0_s,
    c1_s,
    acc_s,
    row_acc,
    col_acc,
    grads_s,
):
    g = pl.program_id(0)
    new = g % 2
    old = 1 - new
    d = s_ref[2 * blocks + 1]
    first = s_ref[2 * blocks] * tiles

    @pl.when(g == 0)
    def _():
        acc_s[...] = jnp.zeros_like(acc_s)
        row_acc[...] = jnp.zeros_like(row_acc)
        col_acc[...] = jnp.zeros_like(col_acc)
        line = lax.broadcasted_iota(jnp.int32, (ROWS, 256), 0)
        lane = lax.broadcasted_iota(jnp.int32, (ROWS, 256), 1)
        r = line // PLANE
        jp = (line % PLANE) // STEP
        s = line % STEP
        ii = lane // 64
        jj = (lane // 32) % 2
        for ig in range(2):
            dist = TILE * d - 64 * ig + 32 * jp + s - r + 16 * (jj - ii)
            dist_s[ig] = jnp.where(dist >= 0, dist, 1 << 20).astype(F32)

    core = s_ref[2 * blocks + 1] % 2

    def codes(n):
        left, right = spread_ref[0], spread_ref[1]

        def chunk(block, h, rows):
            slot = s_ref[jnp.clip(block, 0, blocks - 1)]
            return jnp.where(core == h, mine_ref[slot, rows, :], theirs_ref[slot, rows, :])

        first_half, second_half = (chunk(n, h, slice(0, 32)) for h in range(2))
        return jnp.concatenate(
            [
                dot(chunk(n - 1, 1, slice(16, 32)), right),
                dot(first_half, left),
                dot(first_half, right),
                dot(second_half, left),
                dot(second_half, right),
                dot(chunk(n + 1, 0, slice(0, 16)), left),
            ],
            axis=0,
        )

    def kind(i):
        return 0 if i == 0 else (2 if i == SLABS - 1 else 1)

    def prepare(q):
        here = first + g * TOGETHER + q
        slot = new * TOGETHER + q
        row_codes = codes(here)
        u_row[q] = row_codes[:, :128]
        w_row[slot] = row_codes[:, 128:]
        col_codes = codes(here + d).reshape(SLABS, STEP, 256)
        group = lax.broadcasted_iota(jnp.int32, (STEP, 256), 1) // C % 4
        for jp in range(PAIRS):
            window = col_codes[2 * jp]
            for m in range(1, 4):
                window = jnp.where(group == m, col_codes[2 * jp + m], window)
            uq_s[q, jp * STEP : (jp + 1) * STEP, :] = window[:, :128]
            wq_s[slot, 1, jp * STEP : (jp + 1) * STEP, :] = window[:, 128:]
        line = lax.broadcasted_iota(jnp.int32, (PLANE, 128), 0)
        lane = lax.broadcasted_iota(jnp.int32, (PLANE, 128), 1)
        at_left = (line < STEP) & (lane < C)
        at_right = (line >= PLANE - STEP) & (lane >= 3 * C)
        for k in range(3):
            ar = here - 1 + k

            def inside(cb):
                ok = (ar >= 0) & (ar < blocks) & (cb >= ar) & (cb - ar < BAND) & (cb < blocks)
                return jnp.where(ok, 1.0, 0.0).astype(F32)

            bg = here + d
            mask_s[slot, k] = jnp.where(
                at_left, inside(bg - 1), jnp.where(at_right, inside(bg + 1), inside(bg))
            )
        plain_w = wq_s[slot, 1]
        wq_plain[q] = plain_w
        for k in range(3):
            wq_s[slot, k] = plain_w * mask_s[slot, k]

    def edged(value, which, k):
        mask = mask_s.at[which, k]
        if k != 1:
            return value * mask[...]
        return jnp.concatenate(
            [
                value[:STEP] * mask[:STEP, :],
                value[STEP : PLANE - STEP],
                value[PLANE - STEP :] * mask[PLANE - STEP :, :],
            ],
            axis=0,
        )

    def make_map(q, i, r):
        slot = new * TOGETHER + q
        u = u_row[q, pl.ds(i * STEP + r, 1), :]
        w = w_row[slot, pl.ds(i * STEP + r, 1), :]
        value = edged((u + uq_s[q]) + w * wq_plain[q], slot, kind(i))
        x_s[slot, i, pl.ds(r * PLANE, PLANE), :] = value.astype(BF)

    def make_maps(r, carry):
        for q in range(TOGETHER):
            for i in range(SLABS):
                make_map(q, i, r)
        return carry

    @pl.when(g == 0)
    def _():
        for q in range(TOGETHER):
            prepare(q)
        lax.fori_loop(0, STEP, make_maps, 0)

    bias = vec_ref[0:1, :]
    read = vec_ref[1:2, :]
    half_read = 0.5 * read
    read_density = read * INV_SQRT_TAU
    planes = CHUNK // PLANE

    def tile(q):
        t = (g - 1) * TOGETHER + q
        slot = old * TOGETHER + q
        a = first + t
        b = a + d
        reach = s_ref[blocks + a]
        c0_s[q] = jnp.zeros((PLANE, 128), F32)
        c1_s[q] = jnp.zeros((3, PLANE, 128), F32)

        turned = tgt_ref[t].astype(F32).T.reshape(PAIRS, 2, STEP, TILE)
        sides = [turned[:, jj].reshape(PLANE, TILE) for jj in range(2)]

        def make_target(r):
            for jj in range(2):
                value = sides[jj] if r == 0 else pltpu.roll(sides[jj], TILE - r, 1)
                tgt_s[q, r * PLANE : (r + 1) * PLANE, TILE * jj : TILE * (jj + 1)] = value.astype(BF)

        n = ROWS // CHUNK
        todo = [(ch, ig) for ch in range(n) for ig in range(2)]
        products, parts, grads, flips, sums = {}, {}, {}, {}, {}

        def pair(ch, k):
            rows = pl.ds(ch * CHUNK, CHUNK)
            return jnp.concatenate([x_s[slot, 2 * k + i, rows, :] for i in range(2)], axis=1)

        def forward(m):
            ch, ig = todo[m]

            def first_pair():
                products[ch, 0] = dot(pair(ch, 0), wf_ref[:, 128:])

            def piece(k):
                products[ch, k] = dot(pair(ch, k), wf_ref[...])

            def last_pair():
                products[ch, 4] = dot(pair(ch, 4), wf_ref[:, :128])

            if ig == 0:
                return [first_pair] + [functools.partial(piece, k) for k in (1, 2)]
            return [functools.partial(piece, 3), last_pair]

        def summed(m, begin):
            ch, ig = todo[m]
            rows = slice(begin, begin + PLANE)
            if ig == 0:
                left, right = products[ch, 0][rows], products[ch, 2][rows, :128]
            else:
                left, right = products[ch, 2][rows, 128:], products[ch, 4][rows]
            middle = products[ch, 2 * ig + 1][rows]
            return jnp.concatenate([middle[:, :128] + left, middle[:, 128:] + right], axis=1)

        def slope(m):
            def piece(begin):
                v = summed(m, begin) + bias
                x = v * SQRT_HALF
                read_cdf = half_read * lax.erf(x) + half_read
                value = v * read_cdf
                high = value.astype(BF)
                parts[m, begin] = (
                    high,
                    read_cdf + (read_density * v) * jnp.exp2(v * (v * HALF_LOG2E)),
                )

            return [functools.partial(piece, x) for x in range(0, CHUNK, PLANE)]

        def error(m):
            ch, ig = todo[m]
            farthest = jnp.where(b < blocks, reach, -1).astype(F32)
            out = {}

            def predict(base):
                pieces = [parts[m, base + x] for x in range(0, MPIECE, PLANE)]
                terms = jnp.concatenate(
                    [
                        jnp.concatenate([x[0] for x in pieces], axis=0),
                        tgt_s[q, pl.ds(ch * CHUNK + base, MPIECE), :],
                    ],
                    axis=1,
                )
                out[base] = dot(terms, place_ref[ig])

            def piece(begin):
                base = begin // MPIECE * MPIECE
                keep = dist_s[ig, pl.ds(ch * CHUNK + begin, PLANE), :] <= farthest
                miss = out[base][begin - base : begin - base + PLANE]
                err = jnp.where(keep, miss, 0.0) * TILE ** (-0.5)
                grads[m, begin] = (err * parts[m, begin][1]).astype(BF)

            todo_list = []
            for base in range(0, CHUNK, MPIECE):
                todo_list.append(functools.partial(predict, base))
                if base:
                    todo_list += [
                        functools.partial(piece, x) for x in range(base - MPIECE, base, PLANE)
                    ]
            todo_list += [
                functools.partial(piece, x) for x in range(CHUNK - MPIECE, CHUNK, PLANE)
            ]
            return todo_list

        def joined(m):
            whole = jnp.concatenate([grads[m, x] for x in range(0, CHUNK, PLANE)], axis=0)
            flips[m] = (whole, whole.T)

        def plain(m):
            ch, ig = todo[m]
            part = dot(pick_ref[:, pl.ds(ch * CHUNK, CHUNK)], flips[m][0])
            sums[ig] = part if ch == 0 else sums[ig] + part

        def plain_back():
            zero = jnp.zeros((2 * PLANE, 128), F32)
            four = [sums[0][:, :128], sums[0][:, 128:], sums[1][:, :128], sums[1][:, 128:]]
            four = [zero] + four + [zero]
            middle = None
            for k in range(SLABS // 2):
                both = jnp.concatenate([four[k], four[k + 1]], axis=1)
                high = both.astype(BF)
                low = (both - high.astype(F32)).astype(BF)
                out = dot(high, wb_ref[...]) + dot(low, wb_ref[...])
                for half in range(2):
                    i = 2 * k + half
                    value = out[:, 128 * half : 128 * (half + 1)]
                    rows = value[:PLANE].reshape(PAIRS, STEP, 128)
                    mask = mask_s.at[slot, kind(i)]
                    total = rows[0] * mask[0:1, :] + rows[PAIRS - 1] * mask[PLANE - 1 : PLANE, :]
                    for jp in range(1, PAIRS - 1):
                        total = total + rows[jp] * mask[STEP : STEP + 1, :]
                    here = pl.ds(pl.multiple_of(t * TILE, TILE) + i * STEP, STEP)
                    row_acc[0, here, :] += total
                    if kind(i) == 1:
                        middle = value[PLANE:] if middle is None else middle + value[PLANE:]
                    else:
                        c0_s[q] += value[PLANE:] * mask[...]
            c0_s[q] += middle * mask_s[slot, 1]

        def sides_of(m, which):
            ch, ig = todo[m]
            axis = 1 - which
            take = lambda n, h: lax.slice_in_dim(flips[n][which], 128 * h, 128 * h + 128, axis=axis)
            if ig == 0:
                return [(0, take(m, 0), slice(128, 256)), (1, flips[m][which], slice(0, 256))]
            return [
                (2, jnp.concatenate([take(m - 1, 1), take(m, 0)], axis=axis), slice(0, 256)),
                (3, flips[m][which], slice(0, 256)),
                (4, take(m, 1), slice(0, 128)),
            ]

        def taps(m):
            ch, ig = todo[m]

            def piece(n):
                k, lhs, where = sides_of(m, 1)[n]
                acc_s[where, :] += dot(lhs, pair(ch, k))

            return [functools.partial(piece, n) for n in range(2 + ig)]

        def back(m):
            ch, ig = todo[m]
            totals = {}

            def product(n):
                k, lhs, where = sides_of(m, 0)[n]
                totals[k] = dot(lhs, wb_ref[where, :])

            def piece(k, half, begin):
                i = 2 * k + half
                c1 = c1_s[q, kind(i)]
                wq = wq_s[slot, kind(i)]
                r1 = []
                for rr in range(begin, begin + GROUP):
                    p = i * STEP + ch * planes + rr
                    dx = totals[k][rr * PLANE : (rr + 1) * PLANE, 128 * half : 128 * (half + 1)]
                    c1 = c1 + dx * w_row[slot, p : p + 1, :]
                    r1.append(jnp.sum((dx * wq).reshape(PLANE // 8, 8, 128), axis=0))
                c1_s[q, kind(i)] = c1
                rows = pl.ds(pl.multiple_of(t * TILE, TILE) + i * STEP + ch * planes + begin, 8)
                row_acc[1, rows, :] += rows_of_sums(r1)

            out = []
            for n in range(2 + ig):
                out.append(functools.partial(product, n))
            for n in range(2 + ig):
                k = n + 2 * ig
                out += [
                    functools.partial(piece, k, half, x)
                    for half in range(2)
                    for x in range(0, planes, GROUP)
                ]
            return out

        group = lax.broadcasted_iota(jnp.int32, (STEP, 128), 1) // C

        def unwind(ref):
            pieces = []
            for m in range(PAIRS + 1):
                for odd in range(2):
                    value = jnp.zeros((STEP, 128), F32)
                    if m < PAIRS:
                        value = jnp.where(group == odd, ref[m * STEP : (m + 1) * STEP, :], value)
                    if m > 0:
                        value = jnp.where(
                            group == 2 + odd, ref[(m - 1) * STEP : m * STEP, :], value
                        )
                    pieces.append(value)
            return jnp.concatenate(pieces, axis=0)

        def finish():
            plain_back()
            here = pl.ds(pl.multiple_of(t * TILE, TILE), SPAN)
            c1_s[q, 0] = (
                c1_s[q, 0] * mask_s[slot, 0]
                + c1_s[q, 1] * mask_s[slot, 1]
                + c1_s[q, 2] * mask_s[slot, 2]
            )
            col_acc[0, here, :] += unwind(c0_s.at[q])
            col_acc[1, here, :] += unwind(c1_s.at[q, 0])

        targets = [functools.partial(make_target, r) for r in range(STEP)]

        def step(m):
            out = []
            if 0 <= m < units:
                out.append(forward(m))
            if 0 <= m - 1 < units:
                out.append(slope(m - 1))
            if 0 <= m - 2 < units:
                out.append(error(m - 2))
            if 0 <= m - 3 < units:
                out.append(
                    [functools.partial(joined, m - 3), functools.partial(plain, m - 3)]
                    + taps(m - 3)
                    + back(m - 3)
                    + ([finish] if m - 3 == units - 1 else [])
                )
            if m in (0, 1):
                out.append(targets[STEP * m // 2 : STEP * (m + 1) // 2])
            return out

        units = len(todo)
        return step

    def group_of_tiles():
        for q in range(TOGETHER):
            prepare(q)
        fresh = [
            functools.partial(make_map, q, i, r)
            for q in range(TOGETHER)
            for r in range(STEP)
            for i in range(SLABS)
        ]
        tile_steps = [tile(q) for q in range(TOGETHER)]
        units = 2 * (ROWS // CHUNK)
        steps = units * TOGETHER + 3
        for m in range(steps):
            share = fresh[len(fresh) * m // steps : len(fresh) * (m + 1) // steps]
            lists = [x for q in range(TOGETHER) for x in tile_steps[q](m - units * q)]
            weave(*lists, share)

    @pl.when(g > 0)
    def _():
        group_of_tiles()

    @pl.when(g == tiles // TOGETHER)
    def _():
        grads_s[...] = jnp.zeros_like(grads_s)
        low_half = lax.broadcasted_iota(jnp.int32, (32, 128), 1) < 64
        even = lax.broadcasted_iota(jnp.int32, row_acc.shape[1:], 1) // C % 2 == 0
        for acc_ref in (row_acc, col_acc):
            acc_ref[0] = jnp.where(even, lane_fold(acc_ref[0]), lane_fold(acc_ref[1]))


        def put(acc_ref, base, k, begin, count):
            n = base + k

            @pl.when((n >= 0) & (n < blocks))
            def _():
                slot = s_ref[n]
                for h in range(2):
                    top = acc_ref[0, pl.ds(begin + 64 * h, 32), :]
                    bottom = acc_ref[0, pl.ds(begin + 64 * h + 32, 32), :]
                    grads_s[(h + core) % 2, slot] += jnp.where(low_half, top, bottom)

        for acc_ref, base in ((row_acc, first), (col_acc, first + d)):
            for k in range(tiles):
                put(acc_ref, base, k, STEP + k * TILE, TILE)

            @pl.when((base > 0) & (base <= blocks))
            def _():
                slot = s_ref[jnp.clip(base - 1, 0, blocks - 1)]
                grads_s[(1 + core) % 2, slot, pl.ds(16, 16), :] += jnp.where(
                    low_half[:16], 0.0, acc_ref[0, 0:STEP, :]
                )

            @pl.when(base + tiles < blocks)
            def _():
                slot = s_ref[jnp.minimum(base + tiles, blocks - 1)]
                grads_s[core, slot, pl.ds(0, 16), :] += jnp.where(
                    low_half[:16], acc_ref[0, STEP + tiles * TILE : 2 * STEP + tiles * TILE, :], 0.0
                )

        keep_ref[...] = grads_s[0]
        send_ref[...] = grads_s[1].astype(BF)
        for ty in range(3):
            total = (
                acc_s[64 * (2 - ty) : 64 * (3 - ty), :128]
                + acc_s[64 * (3 - ty) : 64 * (4 - ty), 128:]
            )
            taps_ref[ty] = total[:C] + pltpu.roll(total[C:], 96, 1)


def run_tiles(scalars, mine, theirs, targets, wf, wb, vec, blocks, tiles):
    lane = jnp.arange(256, dtype=jnp.int32)
    source = lane // 128 * C + lane % C
    depth = jnp.arange(128, dtype=jnp.int32)
    spread = jnp.stack(
        [depth[:, None] == source[None, :], depth[:, None] == 64 + source[None, :]]
    ).astype(BF)
    ones = lane[:, None] // C == lane[None, :] // C
    place = jnp.stack(
        [
            jnp.concatenate(
                [ones.astype(BF)]
                + [
                    -(
                        (depth[:, None] == 16 * (4 * ig + lane[None, :] // 64))
                        & (lane[None, :] // C % 2 == jj)
                    ).astype(BF)
                    for jj in range(2)
                ],
                axis=0,
            )
            for ig in range(2)
        ]
    )

    kept = jnp.arange(2 * PLANE, dtype=jnp.int32)[:, None]
    r, jp, s = (x[None, :] for x in (
        jnp.arange(ROWS, dtype=jnp.int32) // PLANE,
        jnp.arange(ROWS, dtype=jnp.int32) % PLANE // STEP,
        jnp.arange(ROWS, dtype=jnp.int32) % STEP,
    ))
    pick = ((kept == jp * STEP + r) | (kept == PLANE + jp * STEP + s)).astype(BF)

    def whole(x):
        zeros = (0,) * x.ndim
        return pl.BlockSpec(x.shape, lambda t, s: zeros)

    grid_spec = pltpu.PrefetchScalarGridSpec(
        num_scalar_prefetch=1,
        grid=(tiles // TOGETHER + 1,),
        in_specs=[
            whole(mine),
            whole(theirs),
            whole(targets),
            whole(wf),
            whole(wb),
            whole(spread),
            whole(place),
            whole(pick),
            whole(vec),
        ],
        out_specs=[
            pl.BlockSpec((blocks, 32, 128), lambda t, s: (0, 0, 0)),
            pl.BlockSpec((blocks, 32, 128), lambda t, s: (0, 0, 0)),
            pl.BlockSpec((3, C, 128), lambda t, s: (0, 0, 0)),
        ],
        scratch_shapes=[
            pltpu.VMEM((TOGETHER, SPAN, 128), F32),
            pltpu.VMEM((2 * TOGETHER, SPAN, 128), F32),
            pltpu.VMEM((TOGETHER, PLANE, 128), F32),
            pltpu.VMEM((2 * TOGETHER, 3, PLANE, 128), F32),
            pltpu.VMEM((TOGETHER, PLANE, 128), F32),
            pltpu.VMEM((2 * TOGETHER, 3, PLANE, 128), F32),
            pltpu.VMEM((2, ROWS, 256), F32),
            pltpu.VMEM((TOGETHER, ROWS, 256), BF),
            pltpu.VMEM((2 * TOGETHER, SLABS, ROWS, 128), BF),
            pltpu.VMEM((TOGETHER, PLANE, 128), F32),
            pltpu.VMEM((TOGETHER, 3, PLANE, 128), F32),
            pltpu.VMEM((256, 256), F32),
            pltpu.VMEM((2, tiles * TILE + 2 * STEP, 128), F32),
            pltpu.VMEM((2, tiles * TILE + 2 * STEP, 128), F32),
            pltpu.VMEM((2, blocks, 32, 128), F32),
        ],
    )
    return pl.pallas_call(
        functools.partial(tile_kernel, blocks, tiles),
        grid_spec=grid_spec,
        out_shape=[
            jax.ShapeDtypeStruct((blocks, 32, 128), F32),
            jax.ShapeDtypeStruct((blocks, 32, 128), BF),
            jax.ShapeDtypeStruct((3, C, 128), F32),
        ],
        compiler_params=pltpu.CompilerParams(
            dimension_semantics=("arbitrary",), vmem_limit_bytes=48 * 1024 * 1024
        ),
    )(
        scalars,
        mine,
        theirs,
        targets,
        wf,
        wb,
        spread,
        place,
        pick,
        vec,
    )


def per_device(
    bins_x,
    proj_weight,
    convolution_weight,
    convolution_bias,
    readout,
    targets,
    block_order,
    band_reach,
):
    tiles = targets.shape[0]
    blocks = block_order.shape[0]
    axes = ("row", "diag")
    code_local = dot(bins_x, proj_weight).astype(BF)
    packed = jnp.concatenate([code_local[:32], code_local[32:]], axis=1)
    core = lax.axis_index("diag") % 2
    peers = lax.axis_size("row") * lax.axis_size("diag")
    same_core = [list(range(c, peers, 2)) for c in range(2)]
    swap = [(i, i ^ 1) for i in range(lax.axis_size("diag"))]
    mine = lax.all_to_all(
        jnp.broadcast_to(packed[None], (blocks, 32, 128)),
        axes,
        0,
        0,
        axis_index_groups=same_core,
        tiled=True,
    )
    theirs = lax.ppermute(mine, "diag", swap)
    positions = jnp.arange(blocks, dtype=jnp.int32)
    inverse = jnp.sum(
        jnp.where(block_order[:, None] == positions[None, :], positions[:, None], 0), axis=0
    )
    scalars = jnp.concatenate(
        [
            inverse,
            band_reach,
            jnp.stack([lax.axis_index("row"), lax.axis_index("diag")]).astype(jnp.int32),
        ]
    )
    taps = convolution_weight.reshape(3, 3, C, C).transpose(0, 1, 3, 2)
    wf = jnp.stack(
        [
            jnp.pad(
                taps[max(0, 2 - rho) : 4 - rho],
                ((max(0, rho - 2), max(0, 1 - rho)), (jj, 1 - jj), (0, 0), (0, 0)),
            )
            for rho in range(4)
            for jj in range(2)
        ],
        axis=3,
    ).reshape(256, 256)
    wb = wf.T
    vec = jnp.stack([jnp.tile(convolution_bias, 8), jnp.tile(readout, 8)])
    keep, send, tap_sums = run_tiles(scalars, mine, theirs, targets, wf, wb, vec, blocks, tiles)
    tap_flat = (
        tap_sums[:, :, : 3 * C].reshape(3, C, 3, C).transpose(0, 2, 1, 3).reshape(2 * blocks, -1)
        / blocks
    )
    owned = tap_flat.shape[1]
    tap_rows = jnp.pad(tap_flat, ((0, 0), (0, 1024 - owned))).reshape(blocks, 2, 8, 128)
    tap_first, tap_second = tap_rows[:, 0], tap_rows[:, 1]
    tap_keep = jnp.where(core == 0, tap_first, tap_second)
    tap_send = jnp.where(core == 0, tap_second, tap_first)
    sent = jnp.concatenate([send, tap_send.astype(BF)], axis=1)
    other = lax.ppermute(sent, "diag", swap)
    terms = jnp.concatenate([keep, tap_keep], axis=1) + other.astype(F32)
    received = lax.all_to_all(
        terms.astype(BF), axes, 0, 0, axis_index_groups=same_core, tiled=True
    )
    total = jnp.sum(received.astype(F32), axis=0)
    codes_grad = jnp.concatenate([total[:32, :64], total[:32, 64:]], axis=0)
    conv_grad = total[32, :owned]
    return (codes_grad, conv_grad)


def solution(mesh):
    in_specs = (P(("row", "diag"), None), P(), P(), P(), P(), P("row", None, "diag"), P(), P())
    out_specs = (P(("row", "diag"), None), P(("row", "diag")))
    return jax.shard_map(
        per_device, mesh=mesh, in_specs=in_specs, out_specs=out_specs, check_vma=False
    )
```

```python
import functools

import jax
import jax.numpy as jnp
from jax import lax
from jax.experimental import pallas as pl
from jax.experimental.pallas import tpu as pltpu
from jax.sharding import PartitionSpec as P

C = 32
TILE = 128
STEP = 16
BAND = 16
PAIRS = TILE // (2 * STEP)
SLABS = TILE // STEP + 2
SPAN = TILE + 2 * STEP
PLANE = PAIRS * STEP
ROWS = STEP * PLANE
CHUNK = 512
MPIECE = 512
GROUP = 8
TOGETHER = 1

SQRT_HALF = 0.7071067811865476
HALF_LOG2E = -0.7213475204444817
INV_SQRT_TAU = 0.3989422804014327
BF = jnp.bfloat16
F32 = jnp.float32


def dot(a, b, dims=(((1,), (0,)), ((), ()))):
    return lax.dot_general(a, b, dims, preferred_element_type=F32)


def rows_of_sums(parts):
    x = [parts[n] for n in (3, 7, 1, 5, 2, 6, 0, 4)]
    s = lax.broadcasted_iota(jnp.int32, (8, 128), 0)
    upper, second, odd = s < 4, s // 2 % 2 == 1, s % 2 == 1
    x = [
        jnp.where(upper, p, q) + pltpu.roll(jnp.where(upper, q, p), 4, 0)
        for p, q in zip(x[0::2], x[1::2])
    ]
    x = [
        jnp.where(second, p + pltpu.roll(p, 2, 0), q + pltpu.roll(q, 6, 0))
        for p, q in zip(x[0::2], x[1::2])
    ]
    p, q = x
    return jnp.where(odd, p + pltpu.roll(p, 1, 0), q + pltpu.roll(q, 7, 0))


def weave(*streams):
    streams = [list(x) for x in streams if x]
    order = sorted(
        ((n + 0.5) / len(x), m, n) for m, x in enumerate(streams) for n in range(len(x))
    )
    for _, m, n in order:
        streams[m][n]()


def tile_kernel(
    blocks,
    tiles,
    s_ref,
    mine_ref,
    theirs_ref,
    tgt_ref,
    wf_ref,
    wb_ref,
    spread_ref,
    place_ref,
    pick_ref,
    vec_ref,
    keep_ref,
    send_ref,
    taps_ref,
    u_row,
    w_row,
    uq_s,
    wq_s,
    wq_plain,
    mask_s,
    dist_s,
    tgt_s,
    x_s,
    c0_s,
    c1_s,
    acc_s,
    row_acc,
    col_acc,
    grads_s,
):
    g = pl.program_id(0)
    new = g % 2
    old = 1 - new
    d = s_ref[2 * blocks + 1]
    first = s_ref[2 * blocks] * tiles

    @pl.when(g == 0)
    def _():
        acc_s[...] = jnp.zeros_like(acc_s)
        row_acc[...] = jnp.zeros_like(row_acc)
        col_acc[...] = jnp.zeros_like(col_acc)
        line = lax.broadcasted_iota(jnp.int32, (ROWS, 256), 0)
        lane = lax.broadcasted_iota(jnp.int32, (ROWS, 256), 1)
        r = line // PLANE
        jp = (line % PLANE) // STEP
        s = line % STEP
        ii = lane // 64
        jj = (lane // 32) % 2
        for ig in range(2):
            dist = TILE * d - 64 * ig + 32 * jp + s - r + 16 * (jj - ii)
            dist_s[ig] = jnp.where(dist >= 0, dist, 1 << 20).astype(F32)

    core = s_ref[2 * blocks + 1] % 2

    def codes(n):
        left, right = spread_ref[0], spread_ref[1]

        def chunk(block, h, rows):
            slot = s_ref[jnp.clip(block, 0, blocks - 1)]
            return jnp.where(core == h, mine_ref[slot, rows, :], theirs_ref[slot, rows, :])

        first_half, second_half = (chunk(n, h, slice(0, 32)) for h in range(2))
        return jnp.concatenate(
            [
                dot(chunk(n - 1, 1, slice(16, 32)), right),
                dot(first_half, left),
                dot(first_half, right),
                dot(second_half, left),
                dot(second_half, right),
                dot(chunk(n + 1, 0, slice(0, 16)), left),
            ],
            axis=0,
        )

    def kind(i):
        return 0 if i == 0 else (2 if i == SLABS - 1 else 1)

    def prepare(q):
        here = first + g * TOGETHER + q
        slot = new * TOGETHER + q
        row_codes = codes(here)
        u_row[q] = row_codes[:, :128]
        w_row[slot] = row_codes[:, 128:]
        col_codes = codes(here + d).reshape(SLABS, STEP, 256)
        group = lax.broadcasted_iota(jnp.int32, (STEP, 256), 1) // C % 4
        for jp in range(PAIRS):
            window = col_codes[2 * jp]
            for m in range(1, 4):
                window = jnp.where(group == m, col_codes[2 * jp + m], window)
            uq_s[q, jp * STEP : (jp + 1) * STEP, :] = window[:, :128]
            wq_s[slot, 1, jp * STEP : (jp + 1) * STEP, :] = window[:, 128:]
        line = lax.broadcasted_iota(jnp.int32, (PLANE, 128), 0)
        lane = lax.broadcasted_iota(jnp.int32, (PLANE, 128), 1)
        at_left = (line < STEP) & (lane < C)
        at_right = (line >= PLANE - STEP) & (lane >= 3 * C)
        for k in range(3):
            ar = here - 1 + k

            def inside(cb):
                ok = (ar >= 0) & (ar < blocks) & (cb >= ar) & (cb - ar < BAND) & (cb < blocks)
                return jnp.where(ok, 1.0, 0.0).astype(F32)

            bg = here + d
            mask_s[slot, k] = jnp.where(
                at_left, inside(bg - 1), jnp.where(at_right, inside(bg + 1), inside(bg))
            )
        plain_w = wq_s[slot, 1]
        wq_plain[q] = plain_w
        for k in range(3):
            wq_s[slot, k] = plain_w * mask_s[slot, k]

    def edged(value, which, k):
        mask = mask_s.at[which, k]
        if k != 1:
            return value * mask[...]
        return jnp.concatenate(
            [
                value[:STEP] * mask[:STEP, :],
                value[STEP : PLANE - STEP],
                value[PLANE - STEP :] * mask[PLANE - STEP :, :],
            ],
            axis=0,
        )

    def make_map(q, i, r):
        slot = new * TOGETHER + q
        u = u_row[q, pl.ds(i * STEP + r, 1), :]
        w = w_row[slot, pl.ds(i * STEP + r, 1), :]
        value = edged((u + uq_s[q]) + w * wq_plain[q], slot, kind(i))
        x_s[slot, i, pl.ds(r * PLANE, PLANE), :] = value.astype(BF)

    def make_maps(r, carry):
        for q in range(TOGETHER):
            for i in range(SLABS):
                make_map(q, i, r)
        return carry

    @pl.when(g == 0)
    def _():
        for q in range(TOGETHER):
            prepare(q)
        lax.fori_loop(0, STEP, make_maps, 0)

    bias = vec_ref[0:1, :]
    read = vec_ref[1:2, :]
    half_read = 0.5 * read
    read_density = read * INV_SQRT_TAU
    planes = CHUNK // PLANE

    def tile(q):
        t = (g - 1) * TOGETHER + q
        slot = old * TOGETHER + q
        a = first + t
        b = a + d
        reach = s_ref[blocks + a]
        c0_s[q] = jnp.zeros((PLANE, 128), F32)
        c1_s[q] = jnp.zeros((3, PLANE, 128), F32)

        turned = tgt_ref[t].astype(F32).T.reshape(PAIRS, 2, STEP, TILE)
        sides = [turned[:, jj].reshape(PLANE, TILE) for jj in range(2)]

        def make_target(r):
            for jj in range(2):
                value = sides[jj] if r == 0 else pltpu.roll(sides[jj], TILE - r, 1)
                tgt_s[q, r * PLANE : (r + 1) * PLANE, TILE * jj : TILE * (jj + 1)] = value.astype(BF)

        n = ROWS // CHUNK
        todo = [(ch, ig) for ch in range(n) for ig in range(2)]
        products, parts, grads, flips, sums = {}, {}, {}, {}, {}

        def pair(ch, k):
            rows = pl.ds(ch * CHUNK, CHUNK)
            return jnp.concatenate([x_s[slot, 2 * k + i, rows, :] for i in range(2)], axis=1)

        def forward(m):
            ch, ig = todo[m]

            def first_pair():
                products[ch, 0] = dot(pair(ch, 0), wf_ref[:, 128:])

            def piece(k):
                products[ch, k] = dot(pair(ch, k), wf_ref[...])

            def last_pair():
                products[ch, 4] = dot(pair(ch, 4), wf_ref[:, :128])

            if ig == 0:
                return [first_pair] + [functools.partial(piece, k) for k in (1, 2)]
            return [functools.partial(piece, 3), last_pair]

        def summed(m, begin):
            ch, ig = todo[m]
            rows = slice(begin, begin + PLANE)
            if ig == 0:
                left, right = products[ch, 0][rows], products[ch, 2][rows, :128]
            else:
                left, right = products[ch, 2][rows, 128:], products[ch, 4][rows]
            middle = products[ch, 2 * ig + 1][rows]
            return jnp.concatenate([middle[:, :128] + left, middle[:, 128:] + right], axis=1)

        def slope(m):
            def piece(begin):
                v = summed(m, begin) + bias
                x = v * SQRT_HALF
                read_cdf = half_read * lax.erf(x) + half_read
                value = v * read_cdf
                high = value.astype(BF)
                parts[m, begin] = (
                    high,
                    read_cdf + (read_density * v) * jnp.exp2(v * (v * HALF_LOG2E)),
                )

            return [functools.partial(piece, x) for x in range(0, CHUNK, PLANE)]

        def error(m):
            ch, ig = todo[m]
            farthest = jnp.where(b < blocks, reach, -1).astype(F32)
            out = {}

            def predict(base):
                pieces = [parts[m, base + x] for x in range(0, MPIECE, PLANE)]
                terms = jnp.concatenate(
                    [
                        jnp.concatenate([x[0] for x in pieces], axis=0),
                        tgt_s[q, pl.ds(ch * CHUNK + base, MPIECE), :],
                    ],
                    axis=1,
                )
                out[base] = dot(terms, place_ref[ig])

            def piece(begin):
                base = begin // MPIECE * MPIECE
                keep = dist_s[ig, pl.ds(ch * CHUNK + begin, PLANE), :] <= farthest
                miss = out[base][begin - base : begin - base + PLANE]
                err = jnp.where(keep, miss, 0.0) * TILE ** (-0.5)
                grads[m, begin] = (err * parts[m, begin][1]).astype(BF)

            todo_list = []
            for base in range(0, CHUNK, MPIECE):
                todo_list.append(functools.partial(predict, base))
                if base:
                    todo_list += [
                        functools.partial(piece, x) for x in range(base - MPIECE, base, PLANE)
                    ]
            todo_list += [
                functools.partial(piece, x) for x in range(CHUNK - MPIECE, CHUNK, PLANE)
            ]
            return todo_list

        def joined(m):
            whole = jnp.concatenate([grads[m, x] for x in range(0, CHUNK, PLANE)], axis=0)
            flips[m] = (whole, whole.T)

        def plain(m):
            ch, ig = todo[m]
            part = dot(pick_ref[:, pl.ds(ch * CHUNK, CHUNK)], flips[m][0])
            sums[ig] = part if ch == 0 else sums[ig] + part

        def plain_back():
            zero = jnp.zeros((2 * PLANE, 128), F32)
            four = [sums[0][:, :128], sums[0][:, 128:], sums[1][:, :128], sums[1][:, 128:]]
            four = [zero] + four + [zero]
            middle = None
            for k in range(SLABS // 2):
                both = jnp.concatenate([four[k], four[k + 1]], axis=1)
                high = both.astype(BF)
                low = (both - high.astype(F32)).astype(BF)
                out = dot(high, wb_ref[...]) + dot(low, wb_ref[...])
                for half in range(2):
                    i = 2 * k + half
                    value = out[:, 128 * half : 128 * (half + 1)]
                    rows = value[:PLANE].reshape(PAIRS, STEP, 128)
                    mask = mask_s.at[slot, kind(i)]
                    total = rows[0] * mask[0:1, :] + rows[PAIRS - 1] * mask[PLANE - 1 : PLANE, :]
                    for jp in range(1, PAIRS - 1):
                        total = total + rows[jp] * mask[STEP : STEP + 1, :]
                    here = pl.ds(pl.multiple_of(t * TILE, TILE) + i * STEP, STEP)
                    row_acc[0, here, :] += total
                    if kind(i) == 1:
                        middle = value[PLANE:] if middle is None else middle + value[PLANE:]
                    else:
                        c0_s[q] += value[PLANE:] * mask[...]
            c0_s[q] += middle * mask_s[slot, 1]

        def sides_of(m, which):
            ch, ig = todo[m]
            axis = 1 - which
            take = lambda n, h: lax.slice_in_dim(flips[n][which], 128 * h, 128 * h + 128, axis=axis)
            if ig == 0:
                return [(0, take(m, 0), slice(128, 256)), (1, flips[m][which], slice(0, 256))]
            return [
                (2, jnp.concatenate([take(m - 1, 1), take(m, 0)], axis=axis), slice(0, 256)),
                (3, flips[m][which], slice(0, 256)),
                (4, take(m, 1), slice(0, 128)),
            ]

        def taps(m):
            ch, ig = todo[m]

            def piece(n):
                k, lhs, where = sides_of(m, 1)[n]
                acc_s[where, :] += dot(lhs, pair(ch, k))

            return [functools.partial(piece, n) for n in range(2 + ig)]

        def back(m):
            ch, ig = todo[m]
            totals = {}

            def product(n):
                k, lhs, where = sides_of(m, 0)[n]
                totals[k] = dot(lhs, wb_ref[where, :])

            def piece(k, half, begin):
                i = 2 * k + half
                c1 = c1_s[q, kind(i)]
                wq = wq_s[slot, kind(i)]
                r1 = []
                for rr in range(begin, begin + GROUP):
                    p = i * STEP + ch * planes + rr
                    dx = totals[k][rr * PLANE : (rr + 1) * PLANE, 128 * half : 128 * (half + 1)]
                    c1 = c1 + dx * w_row[slot, p : p + 1, :]
                    r1.append(jnp.sum((dx * wq).reshape(PLANE // 8, 8, 128), axis=0))
                c1_s[q, kind(i)] = c1
                rows = pl.ds(pl.multiple_of(t * TILE, TILE) + i * STEP + ch * planes + begin, 8)
                row_acc[1, rows, :] += rows_of_sums(r1)

            out = []
            for n in range(2 + ig):
                out.append(functools.partial(product, n))
            for n in range(2 + ig):
                k = n + 2 * ig
                out += [
                    functools.partial(piece, k, half, x)
                    for half in range(2)
                    for x in range(0, planes, GROUP)
                ]
            return out

        group = lax.broadcasted_iota(jnp.int32, (STEP, 128), 1) // C

        def unwind(ref):
            pieces = []
            for m in range(PAIRS + 1):
                for odd in range(2):
                    value = jnp.zeros((STEP, 128), F32)
                    if m < PAIRS:
                        value = jnp.where(group == odd, ref[m * STEP : (m + 1) * STEP, :], value)
                    if m > 0:
                        value = jnp.where(
                            group == 2 + odd, ref[(m - 1) * STEP : m * STEP, :], value
                        )
                    pieces.append(value)
            return jnp.concatenate(pieces, axis=0)

        def finish():
            plain_back()
            here = pl.ds(pl.multiple_of(t * TILE, TILE), SPAN)
            c1_s[q, 0] = (
                c1_s[q, 0] * mask_s[slot, 0]
                + c1_s[q, 1] * mask_s[slot, 1]
                + c1_s[q, 2] * mask_s[slot, 2]
            )
            col_acc[0, here, :] += unwind(c0_s.at[q])
            col_acc[1, here, :] += unwind(c1_s.at[q, 0])

        targets = [functools.partial(make_target, r) for r in range(STEP)]

        def step(m):
            out = []
            if 0 <= m < units:
                out.append(forward(m))
            if 0 <= m - 1 < units:
                out.append(slope(m - 1))
            if 0 <= m - 2 < units:
                out.append(error(m - 2))
            if 0 <= m - 3 < units:
                out.append(
                    [functools.partial(joined, m - 3), functools.partial(plain, m - 3)]
                    + taps(m - 3)
                    + back(m - 3)
                    + ([finish] if m - 3 == units - 1 else [])
                )
            if m in (0, 1):
                out.append(targets[STEP * m // 2 : STEP * (m + 1) // 2])
            return out

        units = len(todo)
        return step

    def group_of_tiles():
        for q in range(TOGETHER):
            prepare(q)
        fresh = [
            functools.partial(make_map, q, i, r)
            for q in range(TOGETHER)
            for r in range(STEP)
            for i in range(SLABS)
        ]
        tile_steps = [tile(q) for q in range(TOGETHER)]
        units = 2 * (ROWS // CHUNK)
        steps = units * TOGETHER + 3
        for m in range(steps):
            share = fresh[len(fresh) * m // steps : len(fresh) * (m + 1) // steps]
            lists = [x for q in range(TOGETHER) for x in tile_steps[q](m - units * q)]
            weave(*lists, share)

    @pl.when(g > 0)
    def _():
        group_of_tiles()

    @pl.when(g == tiles // TOGETHER)
    def _():
        grads_s[...] = jnp.zeros_like(grads_s)
        low_half = lax.broadcasted_iota(jnp.int32, (32, 128), 1) < 64
        even = lax.broadcasted_iota(jnp.int32, row_acc.shape[1:], 1) // C % 2 == 0
        for acc_ref in (row_acc, col_acc):
            plain, scaled = acc_ref[0], acc_ref[1]
            sums = jnp.where(even, plain, scaled) + pltpu.roll(
                jnp.where(even, scaled, plain), 32, 1
            )
            acc_ref[0] = sums + pltpu.roll(sums, 64, 1)

        def put(acc_ref, base, k, begin, count):
            n = base + k

            @pl.when((n >= 0) & (n < blocks))
            def _():
                slot = s_ref[n]
                for h in range(2):
                    top = acc_ref[0, pl.ds(begin + 64 * h, 32), :]
                    bottom = acc_ref[0, pl.ds(begin + 64 * h + 32, 32), :]
                    grads_s[(h + core) % 2, slot] += jnp.where(low_half, top, bottom)

        for acc_ref, base in ((row_acc, first), (col_acc, first + d)):
            for k in range(tiles):
                put(acc_ref, base, k, STEP + k * TILE, TILE)

            @pl.when((base > 0) & (base <= blocks))
            def _():
                slot = s_ref[jnp.clip(base - 1, 0, blocks - 1)]
                grads_s[(1 + core) % 2, slot, pl.ds(16, 16), :] += jnp.where(
                    low_half[:16], 0.0, acc_ref[0, 0:STEP, :]
                )

            @pl.when(base + tiles < blocks)
            def _():
                slot = s_ref[jnp.minimum(base + tiles, blocks - 1)]
                grads_s[core, slot, pl.ds(0, 16), :] += jnp.where(
                    low_half[:16], acc_ref[0, STEP + tiles * TILE : 2 * STEP + tiles * TILE, :], 0.0
                )

        keep_ref[...] = grads_s[0]
        send_ref[...] = grads_s[1].astype(BF)
        for ty in range(3):
            total = (
                acc_s[64 * (2 - ty) : 64 * (3 - ty), :128]
                + acc_s[64 * (3 - ty) : 64 * (4 - ty), 128:]
            )
            taps_ref[ty] = total[:C] + pltpu.roll(total[C:], 96, 1)


def run_tiles(scalars, mine, theirs, targets, wf, wb, vec, blocks, tiles):
    lane = jnp.arange(256, dtype=jnp.int32)
    source = lane // 128 * C + lane % C
    depth = jnp.arange(128, dtype=jnp.int32)
    spread = jnp.stack(
        [depth[:, None] == source[None, :], depth[:, None] == 64 + source[None, :]]
    ).astype(BF)
    ones = lane[:, None] // C == lane[None, :] // C
    place = jnp.stack(
        [
            jnp.concatenate(
                [ones.astype(BF)]
                + [
                    -(
                        (depth[:, None] == 16 * (4 * ig + lane[None, :] // 64))
                        & (lane[None, :] // C % 2 == jj)
                    ).astype(BF)
                    for jj in range(2)
                ],
                axis=0,
            )
            for ig in range(2)
        ]
    )

    kept = jnp.arange(2 * PLANE, dtype=jnp.int32)[:, None]
    r, jp, s = (x[None, :] for x in (
        jnp.arange(ROWS, dtype=jnp.int32) // PLANE,
        jnp.arange(ROWS, dtype=jnp.int32) % PLANE // STEP,
        jnp.arange(ROWS, dtype=jnp.int32) % STEP,
    ))
    pick = ((kept == jp * STEP + r) | (kept == PLANE + jp * STEP + s)).astype(BF)

    def whole(x):
        zeros = (0,) * x.ndim
        return pl.BlockSpec(x.shape, lambda t, s: zeros)

    grid_spec = pltpu.PrefetchScalarGridSpec(
        num_scalar_prefetch=1,
        grid=(tiles // TOGETHER + 1,),
        in_specs=[
            whole(mine),
            whole(theirs),
            whole(targets),
            whole(wf),
            whole(wb),
            whole(spread),
            whole(place),
            whole(pick),
            whole(vec),
        ],
        out_specs=[
            pl.BlockSpec((blocks, 32, 128), lambda t, s: (0, 0, 0)),
            pl.BlockSpec((blocks, 32, 128), lambda t, s: (0, 0, 0)),
            pl.BlockSpec((3, C, 128), lambda t, s: (0, 0, 0)),
        ],
        scratch_shapes=[
            pltpu.VMEM((TOGETHER, SPAN, 128), F32),
            pltpu.VMEM((2 * TOGETHER, SPAN, 128), F32),
            pltpu.VMEM((TOGETHER, PLANE, 128), F32),
            pltpu.VMEM((2 * TOGETHER, 3, PLANE, 128), F32),
            pltpu.VMEM((TOGETHER, PLANE, 128), F32),
            pltpu.VMEM((2 * TOGETHER, 3, PLANE, 128), F32),
            pltpu.VMEM((2, ROWS, 256), F32),
            pltpu.VMEM((TOGETHER, ROWS, 256), BF),
            pltpu.VMEM((2 * TOGETHER, SLABS, ROWS, 128), BF),
            pltpu.VMEM((TOGETHER, PLANE, 128), F32),
            pltpu.VMEM((TOGETHER, 3, PLANE, 128), F32),
            pltpu.VMEM((256, 256), F32),
            pltpu.VMEM((2, tiles * TILE + 2 * STEP, 128), F32),
            pltpu.VMEM((2, tiles * TILE + 2 * STEP, 128), F32),
            pltpu.VMEM((2, blocks, 32, 128), F32),
        ],
    )
    return pl.pallas_call(
        functools.partial(tile_kernel, blocks, tiles),
        grid_spec=grid_spec,
        out_shape=[
            jax.ShapeDtypeStruct((blocks, 32, 128), F32),
            jax.ShapeDtypeStruct((blocks, 32, 128), BF),
            jax.ShapeDtypeStruct((3, C, 128), F32),
        ],
        compiler_params=pltpu.CompilerParams(
            dimension_semantics=("arbitrary",), vmem_limit_bytes=48 * 1024 * 1024
        ),
    )(
        scalars,
        mine,
        theirs,
        targets,
        wf,
        wb,
        spread,
        place,
        pick,
        vec,
    )


def per_device(
    bins_x,
    proj_weight,
    convolution_weight,
    convolution_bias,
    readout,
    targets,
    block_order,
    band_reach,
):
    tiles = targets.shape[0]
    blocks = block_order.shape[0]
    axes = ("row", "diag")
    code_local = dot(bins_x, proj_weight).astype(BF)
    packed = jnp.concatenate([code_local[:32], code_local[32:]], axis=1)
    core = lax.axis_index("diag") % 2
    peers = lax.axis_size("row") * lax.axis_size("diag")
    same_core = [list(range(c, peers, 2)) for c in range(2)]
    swap = [(i, i ^ 1) for i in range(lax.axis_size("diag"))]
    mine = lax.all_to_all(
        jnp.broadcast_to(packed[None], (blocks, 32, 128)),
        axes,
        0,
        0,
        axis_index_groups=same_core,
        tiled=True,
    )
    theirs = lax.ppermute(mine, "diag", swap)
    positions = jnp.arange(blocks, dtype=jnp.int32)
    inverse = jnp.sum(
        jnp.where(block_order[:, None] == positions[None, :], positions[:, None], 0), axis=0
    )
    scalars = jnp.concatenate(
        [
            inverse,
            band_reach,
            jnp.stack([lax.axis_index("row"), lax.axis_index("diag")]).astype(jnp.int32),
        ]
    )
    taps = convolution_weight.reshape(3, 3, C, C).transpose(0, 1, 3, 2)
    wf = jnp.stack(
        [
            jnp.pad(
                taps[max(0, 2 - rho) : 4 - rho],
                ((max(0, rho - 2), max(0, 1 - rho)), (jj, 1 - jj), (0, 0), (0, 0)),
            )
            for rho in range(4)
            for jj in range(2)
        ],
        axis=3,
    ).reshape(256, 256)
    wb = wf.T
    vec = jnp.stack([jnp.tile(convolution_bias, 8), jnp.tile(readout, 8)])
    keep, send, tap_sums = run_tiles(scalars, mine, theirs, targets, wf, wb, vec, blocks, tiles)
    tap_flat = (
        tap_sums[:, :, : 3 * C].reshape(3, C, 3, C).transpose(0, 2, 1, 3).reshape(2 * blocks, -1)
        / blocks
    )
    owned = tap_flat.shape[1]
    tap_rows = jnp.pad(tap_flat, ((0, 0), (0, 1024 - owned))).reshape(blocks, 2, 8, 128)
    tap_first, tap_second = tap_rows[:, 0], tap_rows[:, 1]
    tap_keep = jnp.where(core == 0, tap_first, tap_second)
    tap_send = jnp.where(core == 0, tap_second, tap_first)
    sent = jnp.concatenate([send, tap_send.astype(BF)], axis=1)
    other = lax.ppermute(sent, "diag", swap)
    terms = jnp.concatenate([keep, tap_keep], axis=1) + other.astype(F32)
    received = lax.all_to_all(
        terms.astype(BF), axes, 0, 0, axis_index_groups=same_core, tiled=True
    )
    total = jnp.sum(received.astype(F32), axis=0)
    codes_grad = jnp.concatenate([total[:32, :64], total[:32, 64:]], axis=0)
    conv_grad = total[32, :owned]
    return (codes_grad, conv_grad)


def solution(mesh):
    in_specs = (P(("row", "diag"), None), P(), P(), P(), P(), P("row", None, "diag"), P(), P())
    out_specs = (P(("row", "diag"), None), P(("row", "diag")))
    return jax.shard_map(
        per_device, mesh=mesh, in_specs=in_specs, out_specs=out_specs, check_vma=False
    )
```

```python
import functools

import jax
import jax.numpy as jnp
from jax import lax
from jax.experimental import pallas as pl
from jax.experimental.pallas import tpu as pltpu
from jax.sharding import PartitionSpec as P

C = 32
TILE = 128
STEP = 16
BAND = 16
PAIRS = TILE // (2 * STEP)
SLABS = TILE // STEP + 2
SPAN = TILE + 2 * STEP
PLANE = PAIRS * STEP
ROWS = STEP * PLANE
CHUNK = 512
MPIECE = 512
GROUP = 8
TOGETHER = 1

SQRT_HALF = 0.7071067811865476
HALF_LOG2E = -0.7213475204444817
INV_SQRT_TAU = 0.3989422804014327
BF = jnp.bfloat16
F32 = jnp.float32


def dot(a, b, dims=(((1,), (0,)), ((), ()))):
    return lax.dot_general(a, b, dims, preferred_element_type=F32)


def rows_of_sums(parts):
    x = [parts[n] for n in (3, 7, 1, 5, 2, 6, 0, 4)]
    s = lax.broadcasted_iota(jnp.int32, (8, 128), 0)
    upper, second, odd = s < 4, s // 2 % 2 == 1, s % 2 == 1
    x = [
        jnp.where(upper, p, q) + pltpu.roll(jnp.where(upper, q, p), 4, 0)
        for p, q in zip(x[0::2], x[1::2])
    ]
    x = [
        jnp.where(second, p + pltpu.roll(p, 2, 0), q + pltpu.roll(q, 6, 0))
        for p, q in zip(x[0::2], x[1::2])
    ]
    p, q = x
    return jnp.where(odd, p + pltpu.roll(p, 1, 0), q + pltpu.roll(q, 7, 0))


def weave(*streams):
    streams = [list(x) for x in streams if x]
    order = sorted(
        ((n + 0.5) / len(x), m, n) for m, x in enumerate(streams) for n in range(len(x))
    )
    for _, m, n in order:
        streams[m][n]()


def tile_kernel(
    blocks,
    tiles,
    s_ref,
    mine_ref,
    theirs_ref,
    tgt_ref,
    wf_ref,
    wb_ref,
    spread_ref,
    place_ref,
    pick_ref,
    vec_ref,
    keep_ref,
    send_ref,
    taps_ref,
    u_row,
    w_row,
    uq_s,
    wq_s,
    wq_plain,
    mask_s,
    dist_s,
    tgt_s,
    x_s,
    c0_s,
    c1_s,
    acc_s,
    row_acc,
    col_acc,
    grads_s,
):
    g = pl.program_id(0)
    new = g % 2
    old = 1 - new
    d = s_ref[2 * blocks + 1]
    first = s_ref[2 * blocks] * tiles

    @pl.when(g == 0)
    def _():
        acc_s[...] = jnp.zeros_like(acc_s)
        row_acc[...] = jnp.zeros_like(row_acc)
        col_acc[...] = jnp.zeros_like(col_acc)
        line = lax.broadcasted_iota(jnp.int32, (PLANE, 256), 0)
        lane = lax.broadcasted_iota(jnp.int32, (PLANE, 256), 1)
        jp = line // STEP
        s = line % STEP
        ii = lane // 64
        jj = (lane // 32) % 2
        plane = (TILE * d + 32 * jp + s + 16 * (jj - ii)).astype(F32)
        for ig in range(2):
            for r in range(STEP):
                dist = plane - (64 * ig + r)
                dist_s[ig, r * PLANE : (r + 1) * PLANE, :] = jnp.where(
                    dist >= 0, dist, 1048576.0
                )

    core = s_ref[2 * blocks + 1] % 2

    def codes(n):
        left, right = spread_ref[0], spread_ref[1]

        def chunk(block, h, rows):
            slot = s_ref[jnp.clip(block, 0, blocks - 1)]
            return jnp.where(core == h, mine_ref[slot, rows, :], theirs_ref[slot, rows, :])

        first_half, second_half = (chunk(n, h, slice(0, 32)) for h in range(2))
        return jnp.concatenate(
            [
                dot(chunk(n - 1, 1, slice(16, 32)), right),
                dot(first_half, left),
                dot(first_half, right),
                dot(second_half, left),
                dot(second_half, right),
                dot(chunk(n + 1, 0, slice(0, 16)), left),
            ],
            axis=0,
        )

    def kind(i):
        return 0 if i == 0 else (2 if i == SLABS - 1 else 1)

    def prepare(q):
        here = first + g * TOGETHER + q
        slot = new * TOGETHER + q
        row_codes = codes(here)
        u_row[q] = row_codes[:, :128]
        w_row[slot] = row_codes[:, 128:]
        col_codes = codes(here + d).reshape(SLABS, STEP, 256)
        group = lax.broadcasted_iota(jnp.int32, (STEP, 256), 1) // C % 4
        for jp in range(PAIRS):
            window = col_codes[2 * jp]
            for m in range(1, 4):
                window = jnp.where(group == m, col_codes[2 * jp + m], window)
            uq_s[q, jp * STEP : (jp + 1) * STEP, :] = window[:, :128]
            wq_s[slot, 1, jp * STEP : (jp + 1) * STEP, :] = window[:, 128:]
        line = lax.broadcasted_iota(jnp.int32, (PLANE, 128), 0)
        lane = lax.broadcasted_iota(jnp.int32, (PLANE, 128), 1)
        at_left = (line < STEP) & (lane < C)
        at_right = (line >= PLANE - STEP) & (lane >= 3 * C)
        for k in range(3):
            ar = here - 1 + k

            def inside(cb):
                ok = (ar >= 0) & (ar < blocks) & (cb >= ar) & (cb - ar < BAND) & (cb < blocks)
                return jnp.where(ok, 1.0, 0.0).astype(F32)

            bg = here + d
            mask_s[slot, k] = jnp.where(
                at_left, inside(bg - 1), jnp.where(at_right, inside(bg + 1), inside(bg))
            )
        plain_w = wq_s[slot, 1]
        wq_plain[q] = plain_w
        for k in range(3):
            wq_s[slot, k] = plain_w * mask_s[slot, k]

    def edged(value, which, k):
        mask = mask_s.at[which, k]
        if k != 1:
            return value * mask[...]
        return jnp.concatenate(
            [
                value[:STEP] * mask[:STEP, :],
                value[STEP : PLANE - STEP],
                value[PLANE - STEP :] * mask[PLANE - STEP :, :],
            ],
            axis=0,
        )

    def make_map(q, i, r):
        slot = new * TOGETHER + q
        u = u_row[q, pl.ds(i * STEP + r, 1), :]
        w = w_row[slot, pl.ds(i * STEP + r, 1), :]
        value = edged((u + uq_s[q]) + w * wq_plain[q], slot, kind(i))
        x_s[slot, i, pl.ds(r * PLANE, PLANE), :] = value.astype(BF)

    def make_maps(r, carry):
        for q in range(TOGETHER):
            for i in range(SLABS):
                make_map(q, i, r)
        return carry

    @pl.when(g == 0)
    def _():
        for q in range(TOGETHER):
            prepare(q)
        lax.fori_loop(0, STEP, make_maps, 0)

    bias = vec_ref[0:1, :]
    read = vec_ref[1:2, :]
    half_read = 0.5 * read
    read_density = read * INV_SQRT_TAU
    planes = CHUNK // PLANE

    def tile(q):
        t = (g - 1) * TOGETHER + q
        slot = old * TOGETHER + q
        a = first + t
        b = a + d
        reach = s_ref[blocks + a]
        c0_s[q] = jnp.zeros((PLANE, 128), F32)
        c1_s[q] = jnp.zeros((3, PLANE, 128), F32)

        turned = tgt_ref[t].astype(F32).T.reshape(PAIRS, 2, STEP, TILE)
        sides = [turned[:, jj].reshape(PLANE, TILE) for jj in range(2)]

        def make_target(r):
            for jj in range(2):
                value = sides[jj] if r == 0 else pltpu.roll(sides[jj], TILE - r, 1)
                tgt_s[q, r * PLANE : (r + 1) * PLANE, TILE * jj : TILE * (jj + 1)] = value.astype(BF)

        n = ROWS // CHUNK
        todo = [(ch, ig) for ch in range(n) for ig in range(2)]
        products, parts, grads, flips, sums = {}, {}, {}, {}, {}

        def pair(ch, k):
            rows = pl.ds(ch * CHUNK, CHUNK)
            return jnp.concatenate([x_s[slot, 2 * k + i, rows, :] for i in range(2)], axis=1)

        def forward(m):
            ch, ig = todo[m]

            def first_pair():
                products[ch, 0] = dot(pair(ch, 0), wf_ref[:, 128:])

            def piece(k):
                products[ch, k] = dot(pair(ch, k), wf_ref[...])

            def last_pair():
                products[ch, 4] = dot(pair(ch, 4), wf_ref[:, :128])

            if ig == 0:
                return [first_pair] + [functools.partial(piece, k) for k in (1, 2)]
            return [functools.partial(piece, 3), last_pair]

        def summed(m, begin):
            ch, ig = todo[m]
            rows = slice(begin, begin + PLANE)
            if ig == 0:
                left, right = products[ch, 0][rows], products[ch, 2][rows, :128]
            else:
                left, right = products[ch, 2][rows, 128:], products[ch, 4][rows]
            middle = products[ch, 2 * ig + 1][rows]
            return jnp.concatenate([middle[:, :128] + left, middle[:, 128:] + right], axis=1)

        def slope(m):
            def piece(begin):
                v = summed(m, begin) + bias
                x = v * SQRT_HALF
                read_cdf = half_read * lax.erf(x) + half_read
                value = v * read_cdf
                high = value.astype(BF)
                parts[m, begin] = (
                    high,
                    read_cdf + (read_density * v) * jnp.exp2(v * (v * HALF_LOG2E)),
                )

            return [functools.partial(piece, x) for x in range(0, CHUNK, PLANE)]

        def error(m):
            ch, ig = todo[m]
            farthest = jnp.where(b < blocks, reach, -1).astype(F32)
            out = {}

            def predict(base):
                pieces = [parts[m, base + x] for x in range(0, MPIECE, PLANE)]
                terms = jnp.concatenate(
                    [
                        jnp.concatenate([x[0] for x in pieces], axis=0),
                        tgt_s[q, pl.ds(ch * CHUNK + base, MPIECE), :],
                    ],
                    axis=1,
                )
                out[base] = dot(terms, place_ref[ig])

            def piece(begin):
                base = begin // MPIECE * MPIECE
                keep = dist_s[ig, pl.ds(ch * CHUNK + begin, PLANE), :] <= farthest
                miss = out[base][begin - base : begin - base + PLANE]
                err = jnp.where(keep, miss, 0.0) * TILE ** (-0.5)
                grads[m, begin] = (err * parts[m, begin][1]).astype(BF)

            todo_list = []
            for base in range(0, CHUNK, MPIECE):
                todo_list.append(functools.partial(predict, base))
                if base:
                    todo_list += [
                        functools.partial(piece, x) for x in range(base - MPIECE, base, PLANE)
                    ]
            todo_list += [
                functools.partial(piece, x) for x in range(CHUNK - MPIECE, CHUNK, PLANE)
            ]
            return todo_list

        def joined(m):
            whole = jnp.concatenate([grads[m, x] for x in range(0, CHUNK, PLANE)], axis=0)
            flips[m] = (whole, whole.T)

        def plain(m):
            ch, ig = todo[m]
            part = dot(pick_ref[:, pl.ds(ch * CHUNK, CHUNK)], flips[m][0])
            sums[ig] = part if ch == 0 else sums[ig] + part

        def plain_back():
            zero = jnp.zeros((2 * PLANE, 128), F32)
            four = [sums[0][:, :128], sums[0][:, 128:], sums[1][:, :128], sums[1][:, 128:]]
            four = [zero] + four + [zero]
            middle = None
            for k in range(SLABS // 2):
                both = jnp.concatenate([four[k], four[k + 1]], axis=1)
                high = both.astype(BF)
                low = (both - high.astype(F32)).astype(BF)
                out = dot(high, wb_ref[...]) + dot(low, wb_ref[...])
                for half in range(2):
                    i = 2 * k + half
                    value = out[:, 128 * half : 128 * (half + 1)]
                    rows = value[:PLANE].reshape(PAIRS, STEP, 128)
                    mask = mask_s.at[slot, kind(i)]
                    total = rows[0] * mask[0:1, :] + rows[PAIRS - 1] * mask[PLANE - 1 : PLANE, :]
                    for jp in range(1, PAIRS - 1):
                        total = total + rows[jp] * mask[STEP : STEP + 1, :]
                    here = pl.ds(pl.multiple_of(t * TILE, TILE) + i * STEP, STEP)
                    row_acc[0, here, :] += total
                    if kind(i) == 1:
                        middle = value[PLANE:] if middle is None else middle + value[PLANE:]
                    else:
                        c0_s[q] += value[PLANE:] * mask[...]
            c0_s[q] += middle * mask_s[slot, 1]

        def sides_of(m, which):
            ch, ig = todo[m]
            axis = 1 - which
            take = lambda n, h: lax.slice_in_dim(flips[n][which], 128 * h, 128 * h + 128, axis=axis)
            if ig == 0:
                return [(0, take(m, 0), slice(128, 256)), (1, flips[m][which], slice(0, 256))]
            return [
                (2, jnp.concatenate([take(m - 1, 1), take(m, 0)], axis=axis), slice(0, 256)),
                (3, flips[m][which], slice(0, 256)),
                (4, take(m, 1), slice(0, 128)),
            ]

        def taps(m):
            ch, ig = todo[m]

            def piece(n):
                k, lhs, where = sides_of(m, 1)[n]
                acc_s[where, :] += dot(lhs, pair(ch, k))

            return [functools.partial(piece, n) for n in range(2 + ig)]

        def back(m):
            ch, ig = todo[m]
            totals = {}

            def product(n):
                k, lhs, where = sides_of(m, 0)[n]
                totals[k] = dot(lhs, wb_ref[where, :])

            def piece(k, half, begin):
                i = 2 * k + half
                c1 = c1_s[q, kind(i)]
                wq = wq_s[slot, kind(i)]
                r1 = []
                for rr in range(begin, begin + GROUP):
                    p = i * STEP + ch * planes + rr
                    dx = totals[k][rr * PLANE : (rr + 1) * PLANE, 128 * half : 128 * (half + 1)]
                    c1 = c1 + dx * w_row[slot, p : p + 1, :]
                    r1.append(jnp.sum((dx * wq).reshape(PLANE // 8, 8, 128), axis=0))
                c1_s[q, kind(i)] = c1
                rows = pl.ds(pl.multiple_of(t * TILE, TILE) + i * STEP + ch * planes + begin, 8)
                row_acc[1, rows, :] += rows_of_sums(r1)

            out = []
            for n in range(2 + ig):
                out.append(functools.partial(product, n))
            for n in range(2 + ig):
                k = n + 2 * ig
                out += [
                    functools.partial(piece, k, half, x)
                    for half in range(2)
                    for x in range(0, planes, GROUP)
                ]
            return out

        group = lax.broadcasted_iota(jnp.int32, (STEP, 128), 1) // C

        def unwind(ref):
            pieces = []
            for m in range(PAIRS + 1):
                for odd in range(2):
                    value = jnp.zeros((STEP, 128), F32)
                    if m < PAIRS:
                        value = jnp.where(group == odd, ref[m * STEP : (m + 1) * STEP, :], value)
                    if m > 0:
                        value = jnp.where(
                            group == 2 + odd, ref[(m - 1) * STEP : m * STEP, :], value
                        )
                    pieces.append(value)
            return jnp.concatenate(pieces, axis=0)

        def finish():
            plain_back()
            here = pl.ds(pl.multiple_of(t * TILE, TILE), SPAN)
            c1_s[q, 0] = (
                c1_s[q, 0] * mask_s[slot, 0]
                + c1_s[q, 1] * mask_s[slot, 1]
                + c1_s[q, 2] * mask_s[slot, 2]
            )
            col_acc[0, here, :] += unwind(c0_s.at[q])
            col_acc[1, here, :] += unwind(c1_s.at[q, 0])

        targets = [functools.partial(make_target, r) for r in range(STEP)]

        def step(m):
            out = []
            if 0 <= m < units:
                out.append(forward(m))
            if 0 <= m - 1 < units:
                out.append(slope(m - 1))
            if 0 <= m - 2 < units:
                out.append(error(m - 2))
            if 0 <= m - 3 < units:
                out.append(
                    [functools.partial(joined, m - 3), functools.partial(plain, m - 3)]
                    + taps(m - 3)
                    + back(m - 3)
                    + ([finish] if m - 3 == units - 1 else [])
                )
            if m in (0, 1):
                out.append(targets[STEP * m // 2 : STEP * (m + 1) // 2])
            return out

        units = len(todo)
        return step

    def group_of_tiles():
        for q in range(TOGETHER):
            prepare(q)
        fresh = [
            functools.partial(make_map, q, i, r)
            for q in range(TOGETHER)
            for r in range(STEP)
            for i in range(SLABS)
        ]
        tile_steps = [tile(q) for q in range(TOGETHER)]
        units = 2 * (ROWS // CHUNK)
        steps = units * TOGETHER + 3
        for m in range(steps):
            share = fresh[len(fresh) * m // steps : len(fresh) * (m + 1) // steps]
            lists = [x for q in range(TOGETHER) for x in tile_steps[q](m - units * q)]
            weave(*lists, share)

    @pl.when(g > 0)
    def _():
        group_of_tiles()

    @pl.when(g == tiles // TOGETHER)
    def _():
        grads_s[...] = jnp.zeros_like(grads_s)
        low_half = lax.broadcasted_iota(jnp.int32, (32, 128), 1) < 64
        even = lax.broadcasted_iota(jnp.int32, row_acc.shape[1:], 1) // C % 2 == 0
        for acc_ref in (row_acc, col_acc):
            plain, scaled = acc_ref[0], acc_ref[1]
            sums = jnp.where(even, plain, scaled) + pltpu.roll(
                jnp.where(even, scaled, plain), 32, 1
            )
            acc_ref[0] = sums + pltpu.roll(sums, 64, 1)

        def put(acc_ref, base, k, begin, count):
            n = base + k

            @pl.when((n >= 0) & (n < blocks))
            def _():
                slot = s_ref[n]
                for h in range(2):
                    top = acc_ref[0, pl.ds(begin + 64 * h, 32), :]
                    bottom = acc_ref[0, pl.ds(begin + 64 * h + 32, 32), :]
                    grads_s[(h + core) % 2, slot] += jnp.where(low_half, top, bottom)

        for acc_ref, base in ((row_acc, first), (col_acc, first + d)):
            for k in range(tiles):
                put(acc_ref, base, k, STEP + k * TILE, TILE)

            @pl.when((base > 0) & (base <= blocks))
            def _():
                slot = s_ref[jnp.clip(base - 1, 0, blocks - 1)]
                grads_s[(1 + core) % 2, slot, pl.ds(16, 16), :] += jnp.where(
                    low_half[:16], 0.0, acc_ref[0, 0:STEP, :]
                )

            @pl.when(base + tiles < blocks)
            def _():
                slot = s_ref[jnp.minimum(base + tiles, blocks - 1)]
                grads_s[core, slot, pl.ds(0, 16), :] += jnp.where(
                    low_half[:16], acc_ref[0, STEP + tiles * TILE : 2 * STEP + tiles * TILE, :], 0.0
                )

        keep_ref[...] = grads_s[0]
        send_ref[...] = grads_s[1].astype(BF)
        for ty in range(3):
            total = (
                acc_s[64 * (2 - ty) : 64 * (3 - ty), :128]
                + acc_s[64 * (3 - ty) : 64 * (4 - ty), 128:]
            )
            taps_ref[ty] = total[:C] + pltpu.roll(total[C:], 96, 1)


def run_tiles(scalars, mine, theirs, targets, wf, wb, vec, blocks, tiles):
    lane = jnp.arange(256, dtype=jnp.int32)
    source = lane // 128 * C + lane % C
    depth = jnp.arange(128, dtype=jnp.int32)
    spread = jnp.stack(
        [depth[:, None] == source[None, :], depth[:, None] == 64 + source[None, :]]
    ).astype(BF)
    ones = lane[:, None] // C == lane[None, :] // C
    place = jnp.stack(
        [
            jnp.concatenate(
                [ones.astype(BF)]
                + [
                    -(
                        (depth[:, None] == 16 * (4 * ig + lane[None, :] // 64))
                        & (lane[None, :] // C % 2 == jj)
                    ).astype(BF)
                    for jj in range(2)
                ],
                axis=0,
            )
            for ig in range(2)
        ]
    )

    kept = jnp.arange(2 * PLANE, dtype=jnp.int32)[:, None]
    r, jp, s = (x[None, :] for x in (
        jnp.arange(ROWS, dtype=jnp.int32) // PLANE,
        jnp.arange(ROWS, dtype=jnp.int32) % PLANE // STEP,
        jnp.arange(ROWS, dtype=jnp.int32) % STEP,
    ))
    pick = ((kept == jp * STEP + r) | (kept == PLANE + jp * STEP + s)).astype(BF)

    def whole(x):
        zeros = (0,) * x.ndim
        return pl.BlockSpec(x.shape, lambda t, s: zeros)

    grid_spec = pltpu.PrefetchScalarGridSpec(
        num_scalar_prefetch=1,
        grid=(tiles // TOGETHER + 1,),
        in_specs=[
            whole(mine),
            whole(theirs),
            whole(targets),
            whole(wf),
            whole(wb),
            whole(spread),
            whole(place),
            whole(pick),
            whole(vec),
        ],
        out_specs=[
            pl.BlockSpec((blocks, 32, 128), lambda t, s: (0, 0, 0)),
            pl.BlockSpec((blocks, 32, 128), lambda t, s: (0, 0, 0)),
            pl.BlockSpec((3, C, 128), lambda t, s: (0, 0, 0)),
        ],
        scratch_shapes=[
            pltpu.VMEM((TOGETHER, SPAN, 128), F32),
            pltpu.VMEM((2 * TOGETHER, SPAN, 128), F32),
            pltpu.VMEM((TOGETHER, PLANE, 128), F32),
            pltpu.VMEM((2 * TOGETHER, 3, PLANE, 128), F32),
            pltpu.VMEM((TOGETHER, PLANE, 128), F32),
            pltpu.VMEM((2 * TOGETHER, 3, PLANE, 128), F32),
            pltpu.VMEM((2, ROWS, 256), F32),
            pltpu.VMEM((TOGETHER, ROWS, 256), BF),
            pltpu.VMEM((2 * TOGETHER, SLABS, ROWS, 128), BF),
            pltpu.VMEM((TOGETHER, PLANE, 128), F32),
            pltpu.VMEM((TOGETHER, 3, PLANE, 128), F32),
            pltpu.VMEM((256, 256), F32),
            pltpu.VMEM((2, tiles * TILE + 2 * STEP, 128), F32),
            pltpu.VMEM((2, tiles * TILE + 2 * STEP, 128), F32),
            pltpu.VMEM((2, blocks, 32, 128), F32),
        ],
    )
    return pl.pallas_call(
        functools.partial(tile_kernel, blocks, tiles),
        grid_spec=grid_spec,
        out_shape=[
            jax.ShapeDtypeStruct((blocks, 32, 128), F32),
            jax.ShapeDtypeStruct((blocks, 32, 128), BF),
            jax.ShapeDtypeStruct((3, C, 128), F32),
        ],
        compiler_params=pltpu.CompilerParams(
            dimension_semantics=("arbitrary",), vmem_limit_bytes=48 * 1024 * 1024
        ),
    )(
        scalars,
        mine,
        theirs,
        targets,
        wf,
        wb,
        spread,
        place,
        pick,
        vec,
    )


def per_device(
    bins_x,
    proj_weight,
    convolution_weight,
    convolution_bias,
    readout,
    targets,
    block_order,
    band_reach,
):
    tiles = targets.shape[0]
    blocks = block_order.shape[0]
    axes = ("row", "diag")
    code_local = dot(bins_x, proj_weight).astype(BF)
    packed = jnp.concatenate([code_local[:32], code_local[32:]], axis=1)
    core = lax.axis_index("diag") % 2
    peers = lax.axis_size("row") * lax.axis_size("diag")
    same_core = [list(range(c, peers, 2)) for c in range(2)]
    swap = [(i, i ^ 1) for i in range(lax.axis_size("diag"))]
    mine = lax.all_to_all(
        jnp.broadcast_to(packed[None], (blocks, 32, 128)),
        axes,
        0,
        0,
        axis_index_groups=same_core,
        tiled=True,
    )
    theirs = lax.ppermute(mine, "diag", swap)
    positions = jnp.arange(blocks, dtype=jnp.int32)
    inverse = jnp.sum(
        jnp.where(block_order[:, None] == positions[None, :], positions[:, None], 0), axis=0
    )
    scalars = jnp.concatenate(
        [
            inverse,
            band_reach,
            jnp.stack([lax.axis_index("row"), lax.axis_index("diag")]).astype(jnp.int32),
        ]
    )
    taps = convolution_weight.reshape(3, 3, C, C).transpose(0, 1, 3, 2)
    wf = jnp.stack(
        [
            jnp.pad(
                taps[max(0, 2 - rho) : 4 - rho],
                ((max(0, rho - 2), max(0, 1 - rho)), (jj, 1 - jj), (0, 0), (0, 0)),
            )
            for rho in range(4)
            for jj in range(2)
        ],
        axis=3,
    ).reshape(256, 256)
    wb = wf.T
    vec = jnp.stack([jnp.tile(convolution_bias, 8), jnp.tile(readout, 8)])
    keep, send, tap_sums = run_tiles(scalars, mine, theirs, targets, wf, wb, vec, blocks, tiles)
    tap_flat = (
        tap_sums[:, :, : 3 * C].reshape(3, C, 3, C).transpose(0, 2, 1, 3).reshape(2 * blocks, -1)
        / blocks
    )
    owned = tap_flat.shape[1]
    tap_rows = jnp.pad(tap_flat, ((0, 0), (0, 1024 - owned))).reshape(blocks, 2, 8, 128)
    tap_first, tap_second = tap_rows[:, 0], tap_rows[:, 1]
    tap_keep = jnp.where(core == 0, tap_first, tap_second)
    tap_send = jnp.where(core == 0, tap_second, tap_first)
    sent = jnp.concatenate([send, tap_send.astype(BF)], axis=1)
    other = lax.ppermute(sent, "diag", swap)
    terms = jnp.concatenate([keep, tap_keep], axis=1) + other.astype(F32)
    received = lax.all_to_all(
        terms.astype(BF), axes, 0, 0, axis_index_groups=same_core, tiled=True
    )
    total = jnp.sum(received.astype(F32), axis=0)
    codes_grad = jnp.concatenate([total[:32, :64], total[:32, 64:]], axis=0)
    conv_grad = total[32, :owned]
    return (codes_grad, conv_grad)


def solution(mesh):
    in_specs = (P(("row", "diag"), None), P(), P(), P(), P(), P("row", None, "diag"), P(), P())
    out_specs = (P(("row", "diag"), None), P(("row", "diag")))
    return jax.shard_map(
        per_device, mesh=mesh, in_specs=in_specs, out_specs=out_specs, check_vma=False
    )
```
